512 devices in a mesh: depth: 16 (over y_hi, x), tile: 32 (over y_lo, z, core).
Axes of the slice: x: 4, y: 8 (y_hi: 4, y_lo: 2; y = y_hi * 2 + y_lo), z: 8, core: 2. Of those that a mesh axis runs over, the one named last changes fastest.
Arguments:
- volume: float32 [128, 256, 256], P('depth', 'tile'), may hold values from 0.01 to 4
- measured: float32 [128, 256, 256], P('depth', 'tile'), may hold values from 0.3 to 3
- point_spread: bfloat16 [11, 11, 128, 128], replicated, may hold values from 1.5625e-05 to 0.28125
Outputs:
- updated: float32 [128, 256, 256], P('depth', 'tile')
The draws below stay inside these ranges and needn't reach their ends.
All inputs are finite; a program needn't handle non-finite values.
Results may differ from the reference program's by a relative error of at most 0.0008.
Values may be sent and summed in bfloat16 or wider, within the bound.
No kernel may reach another device: no remote copies, remote signals or barrier semaphores. Data moves between devices by JAX's collectives and lax.ppermute only.
A program may use at most 64 MiB of HBM per device.

```python
import math
import jax
import jax.numpy as jnp
from jax import lax

VIEWS = 128
PSF_RADIUS = 5
NX = 256
PLANES = 128
NY = 256


def log_spread(key, full_shape, lowest, highest):
    return jnp.exp(jax.random.uniform(key, full_shape, jnp.float32, math.log(lowest), math.log(highest)))


def draw_volume(key, part):
    key_list = jax.random.split(jax.random.fold_in(key, 7), 3)
    full_shape = (PLANES, NY, NX)
    bead_picks = jax.random.randint(key_list[0], full_shape, 0, 50)
    background = log_spread(key_list[1], full_shape, 0.02, 0.08)
    bright = log_spread(key_list[2], full_shape, 1.0, 3.0)
    return jnp.where(bead_picks == 0, bright, background).astype(jnp.float32)


def draw_point_spread(key, part):
    extent = 2 * PSF_RADIUS + 1
    key_list = jax.random.split(jax.random.fold_in(key, 13), 4)
    view_tilt = jax.random.uniform(key_list[0], (2, 1, VIEWS), jnp.float32, -1.0, 1.0)
    jitter = jax.random.uniform(key_list[1], (PLANES,), jnp.float32, -0.5, 0.5)
    levels = ((jnp.arange(PLANES, dtype=jnp.float32) + 0.5 + jitter) * 2.0 / PLANES - 1.0)[:, None]
    centers = (PSF_RADIUS - 0.5) * levels[None] * view_tilt
    blob_width = 0.35 + 0.45 * jnp.abs(levels)
    offsets = (jnp.arange(extent, dtype=jnp.float32) - PSF_RADIUS)[:, None, None]
    row_part = jnp.exp(-0.5 * ((offsets - centers[0][None]) / blob_width[None]) ** 2)
    col_part = jnp.exp(-0.5 * ((offsets - centers[1][None]) / blob_width[None]) ** 2)
    blob_shape = row_part[:, None] * col_part[None, :]
    blob_shape = blob_shape / jnp.sum(blob_shape, axis=(0, 1), keepdims=True)
    amplitude = log_spread(key_list[2], (PLANES, VIEWS), 0.5, 2.0)
    texture = log_spread(key_list[3], (extent, extent, PLANES, VIEWS), 0.7, 1.4)
    spread_kernel = 12.5 / PLANES * amplitude[None, None] * texture * (blob_shape + 0.0005)
    return spread_kernel.astype(jnp.bfloat16)


def block_scale(rng, shape, pieces, least, high):
    def one(position, shards_of):
        draws = jax.random.uniform(jax.random.fold_in(jax.random.fold_in(rng, 6), position), (shards_of,), jnp.float32, least / len(pieces), high / len(pieces))
        return jnp.repeat(jnp.exp(draws), shape[position] // shards_of).reshape((-1,) + (1,) * (len(shape) - position - 1))

    level = one(*pieces[0])
    for cut in pieces[1:]:
        level = level * one(*cut)
    return level


def setup_inputs(seed: int = 0) -> dict:
    keys = jax.random.split(jax.random.key(seed), 4)
    return {
        "volume": draw_volume(jax.random.fold_in(keys[3], 71), 0),
        "measured": jnp.clip(jnp.exp(math.log(3.0) - 2.3025851 * jax.random.uniform(keys[1], (VIEWS, NY, NX), jnp.float32) ** block_scale(keys[1], (VIEWS, NY, NX), ((0, 16), (1, 32)), -0.2, 0.2)), 0.3, 3.0),
        "point_spread": draw_point_spread(jax.random.fold_in(keys[3], 71), 0),
    }


def reference(volume, measured, point_spread):
    extent = 2 * PSF_RADIUS + 1
    height = volume.shape[1]
    breadth = volume.shape[2]
    kernel = point_spread.astype(jnp.float32)
    volume_low = volume.astype(jnp.bfloat16)
    volume_low = lax.optimization_barrier(volume_low).astype(jnp.float32)
    padded = jnp.pad(volume_low, ((0, 0), (PSF_RADIUS, PSF_RADIUS), (PSF_RADIUS, PSF_RADIUS)))
    projection = jnp.zeros(measured.shape, jnp.float32)
    for row_shift in range(extent):
        for col_shift in range(extent):
            window = padded[:, row_shift:row_shift + height, col_shift:col_shift + breadth]
            projection = projection + jnp.einsum("zyx,zv->vyx", window, kernel[row_shift, col_shift], precision=lax.Precision.HIGHEST)
    ratio = (measured / projection).astype(jnp.bfloat16)
    ratio = lax.optimization_barrier(ratio).astype(jnp.float32)
    padded_ratio = jnp.pad(ratio, ((0, 0), (PSF_RADIUS, PSF_RADIUS), (PSF_RADIUS, PSF_RADIUS)))
    back_sum = jnp.zeros(volume.shape, jnp.float32)
    for row_shift in range(extent):
        for col_shift in range(extent):
            window = padded_ratio[:, row_shift:row_shift + height, col_shift:col_shift + breadth]
            tap_weights = kernel[extent - 1 - row_shift, extent - 1 - col_shift]
            back_sum = back_sum + jnp.einsum("vyx,zv->zyx", window, tap_weights, precision=lax.Precision.HIGHEST)
    weight = jnp.sum(kernel, axis=(0, 1, 3))
    return volume * back_sum / weight[:, None, None]
```

```python
import jax
import jax.numpy as jnp
from jax import lax
from jax.experimental import pallas as pl
from jax.experimental.pallas import tpu as pltpu
from jax.sharding import PartitionSpec as P

R = 5
E = 11
Z = 128
TILES = 16
W = 16
H = 8
S = 32
F32 = jnp.float32
BF16 = jnp.bfloat16
VM = pl.BlockSpec(memory_space=pltpu.VMEM)
PARAMS = pltpu.CompilerParams(vmem_limit_bytes=40 * 1024 * 1024)


def lanes(shape=(8, 128)):
    return lax.broadcasted_iota(jnp.int32, shape, 1)


def pack_kernel(vol_ref, meas_ref, out_ref):
    lane = lanes()
    slot = lane // S
    inside = lane % S
    rolled = {}

    def turned(ref, key, y, half, shift):
        name = (key, y, half, shift % 128)
        if name not in rolled:
            part = ref[:, y, half * 128 : half * 128 + 128]
            rolled[name] = pltpu.roll(part, shift % 128, 1) if shift % 128 else part
        return rolled[name]

    def window(t, y):
        start = W * t - R
        shift = S * (y % 4) - start
        low, high = max(start, 0) // 128, min(start + W + 2 * R - 1, 255) // 128
        value = turned(vol_ref, 0, y, low, shift)
        if high != low:
            value = jnp.where(inside < 128 - start, value, turned(vol_ref, 0, y, high, shift))
        if start < 0:
            value = jnp.where(inside < -start, 0.0, value)
        if start + W + 2 * R > 256:
            value = jnp.where(inside < 256 - start, value, 0.0)
        return value

    for t in range(TILES):
        for g in range(2):
            value = window(t, 4 * g)
            for s in range(1, 4):
                value = jnp.where(slot < s, value, window(t, 4 * g + s))
            out_ref[t, :, g * 128 : g * 128 + 128] = value.astype(BF16)
        value = turned(meas_ref, 1, 0, t // 8, -W * t)
        for y in range(1, H):
            value = jnp.where(lane < W * y, value, turned(meas_ref, 1, y, t // 8, W * y - W * t))
        head = value.astype(BF16)
        out_ref[t, :, 256:384] = head
        out_ref[t, :, 384:512] = (value - head.astype(F32)).astype(BF16)


def ratio_kernel(own_ref, up_ref, down_ref, psf_ref, out_ref, rows_ref, taps_ref):
    def group(ref, g):
        return ref[:, :, g * 128 : g * 128 + 128].astype(F32).reshape(Z, 128)

    lane = lanes((Z, 128))
    mixed = jnp.where(lane < S, group(down_ref, 1), group(up_ref, 0))
    blocks = [mixed, group(up_ref, 1), group(own_ref, 0), group(own_ref, 1), group(down_ref, 0)]
    for i, block in enumerate(blocks):
        rows_ref[i * 128 : i * 128 + 128, :] = block.T
    for y in range(H + 2 * R):
        at = S * ((3 + y) % 20)
        for b in range(E):
            taps_ref[y * W : y * W + W, b * 128 : b * 128 + 128] = rows_ref[at + b : at + b + W, :].astype(BF16)
    total = jnp.zeros((H * W, Z), F32)
    for a in range(E):
        total = total + jnp.dot(
            taps_ref[a * W : a * W + H * W, :], psf_ref[a].reshape(E * Z, Z), preferred_element_type=F32
        )
    measured = (group(own_ref, 2) + group(own_ref, 3)).T
    out_ref[...] = (measured / total).astype(BF16)


def back_kernel(own_ref, up_ref, down_ref, psf_ref, out_ref, rows_ref, taps_ref):
    rows = H + 2 * R
    pitch = 48
    zeros = jnp.zeros((16, 128), F32)
    for y in range(rows):
        if y < R:
            value = up_ref[(y + H - R) * W : (y + H - R) * W + W, :]
        elif y < R + H:
            value = own_ref[(y - R) * W : (y - R) * W + W, :]
        else:
            value = down_ref[(y - R - H) * W : (y - R - H) * W + W, :]
        rows_ref[y * pitch : y * pitch + 16, :] = zeros
        rows_ref[y * pitch + 16 : y * pitch + 32, :] = value.astype(F32)
        rows_ref[y * pitch + 32 : y * pitch + 48, :] = zeros
    last = lax.broadcasted_iota(jnp.int32, (S, 128), 0) == S - 1
    for y in range(rows):
        for b in range(E):
            start = y * pitch + 16 - b
            value = jnp.where(last, 1.0, rows_ref[start : start + S, :])
            taps_ref[y * S : y * S + S, b * 128 : b * 128 + 128] = value.astype(BF16)
    total = jnp.zeros((Z, H * S), F32)
    for a in range(E):
        kernel = jnp.concatenate([psf_ref[a, b] for b in range(E)], axis=1)
        start = (2 * R - a) * S
        total = total + lax.dot_general(
            kernel, taps_ref[start : start + H * S, :], (((1,), (1,)), ((), ())), preferred_element_type=F32
        )
    out_ref[...] = total.reshape(TILES, 8, H * S)


def final_kernel(parts_ref, vol_ref, out_ref):
    lane = lanes()
    weight = parts_ref[0, :, S - 1 : S]

    for y in range(H):
        g, s = y // 4, y % 4
        turned = []
        for t in range(TILES):
            part = parts_ref[t, :, g * 128 : g * 128 + 128]
            shift = (W * t - R - S * s) % 128
            turned.append(pltpu.roll(part, shift, 1) if shift else part)
        for half in range(2):
            sums = [None, None]
            for t in range(TILES):
                start, stop = W * t - R - 128 * half, W * t + W + R - 128 * half
                start, stop = max(start, 0), min(stop, 128)
                if start >= stop:
                    continue
                before = sums[t % 2]
                sums[t % 2] = jnp.where(
                    (lane >= start) & (lane < stop), turned[t], 0.0 if before is None else before
                )
            here = slice(half * 128, half * 128 + 128)
            out_ref[:, y, here] = vol_ref[:, y, here] * (sums[0] + sums[1]) / weight


def both_ways(x, axis):
    count = lax.axis_size(axis)
    down = lax.ppermute(x, axis, [(i, i + 1) for i in range(count - 1)])
    up = lax.ppermute(x, axis, [(i + 1, i) for i in range(count - 1)])
    return down, up


def body(volume, measured, point_spread):
    packed = pl.pallas_call(
        pack_kernel,
        out_shape=jax.ShapeDtypeStruct((TILES, 8, 512), BF16),
        in_specs=[VM, VM],
        out_specs=VM,
        compiler_params=PARAMS,
        name="pack",
    )(volume, measured)
    own = lax.all_to_all(packed, "depth", 0, 0, tiled=True)
    above, below = both_ways(own[:, :, :256], "tile")
    ratio = pl.pallas_call(
        ratio_kernel,
        out_shape=jax.ShapeDtypeStruct((H * W, Z), BF16),
        in_specs=[VM] * 4,
        out_specs=VM,
        scratch_shapes=[
            pltpu.VMEM((5 * 128, 128), F32),
            pltpu.VMEM(((H + 2 * R) * W, E * Z), BF16),
        ],
        compiler_params=PARAMS,
        name="ratio",
    )(own, above, below, point_spread)
    above, below = both_ways(ratio, "tile")
    shares = pl.pallas_call(
        back_kernel,
        out_shape=jax.ShapeDtypeStruct((TILES, 8, H * S), F32),
        in_specs=[VM] * 4,
        out_specs=VM,
        scratch_shapes=[
            pltpu.VMEM(((H + 2 * R) * 48, 128), F32),
            pltpu.VMEM(((H + 2 * R) * S, E * Z), BF16),
        ],
        compiler_params=PARAMS,
        name="back",
    )(ratio, above, below, point_spread)
    parts = lax.all_to_all(shares, "depth", 0, 0, tiled=True)
    return pl.pallas_call(
        final_kernel,
        out_shape=jax.ShapeDtypeStruct(volume.shape, F32),
        in_specs=[VM, VM],
        out_specs=VM,
        compiler_params=PARAMS,
        name="final",
    )(parts, volume)


def solution(mesh):
    in_specs = (P("depth", "tile", None), P("depth", "tile", None), P())
    out_specs = P("depth", "tile", None)
    return jax.shard_map(body, mesh=mesh, in_specs=in_specs, out_specs=out_specs, check_vma=False)
```

```python
import jax
import jax.numpy as jnp
from jax import lax
from jax.experimental import pallas as pl
from jax.experimental.pallas import tpu as pltpu
from jax.sharding import PartitionSpec as P

R = 5
E = 11
Z = 128
TILES = 16
W = 16
H = 8
S = 32
F32 = jnp.float32
BF16 = jnp.bfloat16
VM = pl.BlockSpec(memory_space=pltpu.VMEM)
HBM = pl.BlockSpec(memory_space=pl.ANY)
PARAMS = pltpu.CompilerParams(vmem_limit_bytes=40 * 1024 * 1024)


def lanes(shape=(8, 128)):
    return lax.broadcasted_iota(jnp.int32, shape, 1)


def pack_kernel(vol_hbm, meas_hbm, out_ref, vol_ref, meas_ref, sems):
    copies = [
        pltpu.make_async_copy(vol_hbm, vol_ref, sems.at[0]),
        pltpu.make_async_copy(meas_hbm, meas_ref, sems.at[1]),
    ]
    for copy in copies:
        copy.start()
    copies[0].wait()
    lane = lanes()
    slot = lane // S
    inside = lane % S
    rolled = {}

    def turned(ref, key, y, half, shift):
        name = (key, y, half, shift % 128)
        if name not in rolled:
            part = ref[:, y, half * 128 : half * 128 + 128]
            rolled[name] = pltpu.roll(part, shift % 128, 1) if shift % 128 else part
        return rolled[name]

    def window(t, y):
        start = W * t - R
        shift = S * (y % 4) - start
        low, high = max(start, 0) // 128, min(start + W + 2 * R - 1, 255) // 128
        value = turned(vol_ref, 0, y, low, shift)
        if high != low:
            value = jnp.where(inside < 128 - start, value, turned(vol_ref, 0, y, high, shift))
        if start < 0:
            value = jnp.where(inside < -start, 0.0, value)
        if start + W + 2 * R > 256:
            value = jnp.where(inside < 256 - start, value, 0.0)
        return value

    for t in range(TILES):
        for g in range(2):
            value = window(t, 4 * g)
            for s in range(1, 4):
                value = jnp.where(slot < s, value, window(t, 4 * g + s))
            out_ref[t, :, g * 128 : g * 128 + 128] = value.astype(BF16)
    copies[1].wait()
    for t in range(TILES):
        value = turned(meas_ref, 1, 0, t // 8, -W * t)
        for y in range(1, H):
            value = jnp.where(lane < W * y, value, turned(meas_ref, 1, y, t // 8, W * y - W * t))
        head = value.astype(BF16)
        out_ref[t, :, 256:384] = head
        out_ref[t, :, 384:512] = (value - head.astype(F32)).astype(BF16)


def ratio_kernel(own_ref, mate_ref, next_ref, psf_ref, out_ref, rows_ref, taps_ref):
    def group(ref, g):
        return ref[:, :, g * 128 : g * 128 + 128].astype(F32).reshape(Z, 128)

    even = lax.axis_index("tile") % 2 == 0

    def above(g):
        return jnp.where(even, group(next_ref, g), group(mate_ref, g))

    def below(g):
        return jnp.where(even, group(mate_ref, g), group(next_ref, g))

    lane = lanes((Z, 128))
    mixed = jnp.where(lane < S, below(1), above(0))
    blocks = [mixed, above(1), group(own_ref, 0), group(own_ref, 1), below(0)]
    for i, block in enumerate(blocks):
        rows_ref[i * 128 : i * 128 + 128, :] = block.T
    for y in range(H + 2 * R):
        at = S * ((3 + y) % 20)
        for b in range(E):
            taps_ref[y * W : y * W + W, b * 128 : b * 128 + 128] = rows_ref[at + b : at + b + W, :].astype(BF16)
    total = jnp.zeros((H * W, Z), F32)
    for a in range(E):
        total = total + jnp.dot(
            taps_ref[a * W : a * W + H * W, :], psf_ref[a].reshape(E * Z, Z), preferred_element_type=F32
        )
    measured = (group(own_ref, 2) + group(own_ref, 3)).T
    out_ref[...] = (measured / total).astype(BF16)


def back_kernel(own_ref, mate_ref, next_ref, psf_ref, out_ref, rows_ref, taps_ref):
    rows = H + 2 * R
    pitch = 48
    zeros = jnp.zeros((16, 128), F32)
    even = lax.axis_index("tile") % 2 == 0
    for y in range(rows):
        if y < R:
            here = slice((y + H - R) * W, (y + H - R) * W + W)
            value = jnp.where(even, next_ref[here, :].astype(F32), mate_ref[here, :].astype(F32))
        elif y < R + H:
            value = own_ref[(y - R) * W : (y - R) * W + W, :]
        else:
            here = slice((y - R - H) * W, (y - R - H) * W + W)
            value = jnp.where(even, mate_ref[here, :].astype(F32), next_ref[here, :].astype(F32))
        rows_ref[y * pitch : y * pitch + 16, :] = zeros
        rows_ref[y * pitch + 16 : y * pitch + 32, :] = value.astype(F32)
        rows_ref[y * pitch + 32 : y * pitch + 48, :] = zeros
    last = lax.broadcasted_iota(jnp.int32, (S, 128), 0) == S - 1
    for y in range(rows):
        for b in range(E):
            start = y * pitch + 16 - b
            value = jnp.where(last, 1.0, rows_ref[start : start + S, :])
            taps_ref[y * S : y * S + S, b * 128 : b * 128 + 128] = value.astype(BF16)
    total = jnp.zeros((Z, H * S), F32)
    for a in range(E):
        kernel = jnp.concatenate([psf_ref[a, b] for b in range(E)], axis=1)
        start = (2 * R - a) * S
        total = total + lax.dot_general(
            kernel, taps_ref[start : start + H * S, :], (((1,), (1,)), ((), ())), preferred_element_type=F32
        )
    out_ref[...] = total.reshape(TILES, 8, H * S)


def final_kernel(parts_ref, vol_ref, out_ref):
    lane = lanes()
    weight = parts_ref[0, :, S - 1 : S]

    for y in range(H):
        g, s = y // 4, y % 4
        turned = []
        for t in range(TILES):
            part = parts_ref[t, :, g * 128 : g * 128 + 128]
            shift = (W * t - R - S * s) % 128
            turned.append(pltpu.roll(part, shift, 1) if shift else part)
        for half in range(2):
            sums = [None, None]
            for t in range(TILES):
                start, stop = W * t - R - 128 * half, W * t + W + R - 128 * half
                start, stop = max(start, 0), min(stop, 128)
                if start >= stop:
                    continue
                before = sums[t % 2]
                sums[t % 2] = jnp.where(
                    (lane >= start) & (lane < stop), turned[t], 0.0 if before is None else before
                )
            here = slice(half * 128, half * 128 + 128)
            out_ref[:, y, here] = vol_ref[:, y, here] * (sums[0] + sums[1]) / weight


def neighbours(x):
    count = lax.axis_size("tile")
    chips = [(i, i + 1) for i in range(1, count - 1, 2)] + [(i, i - 1) for i in range(2, count, 2)]
    cores = [(i, i + 1) for i in range(0, count, 2)] + [(i, i - 1) for i in range(1, count, 2)]
    return lax.ppermute(x, "tile", cores), lax.ppermute(x, "tile", chips)


def body(volume, measured, point_spread):
    packed = pl.pallas_call(
        pack_kernel,
        out_shape=jax.ShapeDtypeStruct((TILES, 8, 512), BF16),
        in_specs=[HBM] * 2,
        out_specs=VM,
        scratch_shapes=[
            pltpu.VMEM(volume.shape, F32),
            pltpu.VMEM(measured.shape, F32),
            pltpu.SemaphoreType.DMA((2,)),
        ],
        compiler_params=pltpu.CompilerParams(vmem_limit_bytes=56 * 1024 * 1024),
        cost_estimate=pl.CostEstimate(flops=20_000_000_000, bytes_accessed=2**20, transcendentals=0),
        name="pack",
    )(volume, measured)
    own = lax.all_to_all(packed, "depth", 0, 0, tiled=True)
    mate, beyond = neighbours(own[:, :, :256])
    ratio = pl.pallas_call(
        ratio_kernel,
        out_shape=jax.ShapeDtypeStruct((H * W, Z), BF16),
        in_specs=[VM] * 4,
        out_specs=VM,
        scratch_shapes=[
            pltpu.VMEM((5 * 128, 128), F32),
            pltpu.VMEM(((H + 2 * R) * W, E * Z), BF16),
        ],
        compiler_params=PARAMS,
        name="ratio",
    )(own, mate, beyond, point_spread)
    mate, beyond = neighbours(ratio)
    shares = pl.pallas_call(
        back_kernel,
        out_shape=jax.ShapeDtypeStruct((TILES, 8, H * S), F32),
        in_specs=[VM] * 4,
        out_specs=VM,
        scratch_shapes=[
            pltpu.VMEM(((H + 2 * R) * 48, 128), F32),
            pltpu.VMEM(((H + 2 * R) * S, E * Z), BF16),
        ],
        compiler_params=PARAMS,
        name="back",
    )(ratio, mate, beyond, point_spread)
    parts = lax.all_to_all(shares, "depth", 0, 0, tiled=True)
    return pl.pallas_call(
        final_kernel,
        out_shape=jax.ShapeDtypeStruct(volume.shape, F32),
        in_specs=[VM, VM],
        out_specs=VM,
        compiler_params=PARAMS,
        name="final",
    )(parts, volume)


def solution(mesh):
    in_specs = (P("depth", "tile", None), P("depth", "tile", None), P())
    out_specs = P("depth", "tile", None)
    return jax.shard_map(body, mesh=mesh, in_specs=in_specs, out_specs=out_specs, check_vma=False)
```

```python
import jax
import jax.numpy as jnp
from jax import lax
from jax.experimental import pallas as pl
from jax.experimental.pallas import tpu as pltpu
from jax.sharding import PartitionSpec as P

R = 5
E = 11
Z = 128
TILES = 16
W = 16
H = 8
S = 32
F32 = jnp.float32
BF16 = jnp.bfloat16
VM = pl.BlockSpec(memory_space=pltpu.VMEM)
HBM = pl.BlockSpec(memory_space=pl.ANY)
PARAMS = pltpu.CompilerParams(vmem_limit_bytes=40 * 1024 * 1024)


def lanes(shape=(8, 128)):
    return lax.broadcasted_iota(jnp.int32, shape, 1)


def pack_kernel(vol_hbm, meas_hbm, out_ref, vol_ref, meas_ref, sems):
    copies = [
        pltpu.make_async_copy(vol_hbm, vol_ref, sems.at[0]),
        pltpu.make_async_copy(meas_hbm, meas_ref, sems.at[1]),
    ]
    for copy in copies:
        copy.start()
    copies[0].wait()
    lane = lanes()
    slot = lane // S
    inside = lane % S
    rolled = {}

    def turned(ref, key, y, half, shift):
        name = (key, y, half, shift % 128)
        if name not in rolled:
            part = ref[:, y, half * 128 : half * 128 + 128]
            rolled[name] = pltpu.roll(part, shift % 128, 1) if shift % 128 else part
        return rolled[name]

    def window(t, y):
        start = W * t - R
        shift = S * (y % 4) - start
        low, high = max(start, 0) // 128, min(start + W + 2 * R - 1, 255) // 128
        value = turned(vol_ref, 0, y, low, shift)
        if high != low:
            value = jnp.where(inside < 128 - start, value, turned(vol_ref, 0, y, high, shift))
        if start < 0:
            value = jnp.where(inside < -start, 0.0, value)
        if start + W + 2 * R > 256:
            value = jnp.where(inside < 256 - start, value, 0.0)
        return value

    for t in range(TILES):
        for g in range(2):
            value = window(t, 4 * g)
            for s in range(1, 4):
                value = jnp.where(slot < s, value, window(t, 4 * g + s))
            out_ref[t, :, g * 128 : g * 128 + 128] = value.astype(BF16)
    copies[1].wait()
    for t in range(TILES):
        value = turned(meas_ref, 1, 0, t // 8, -W * t)
        for y in range(1, H):
            value = jnp.where(lane < W * y, value, turned(meas_ref, 1, y, t // 8, W * y - W * t))
        head = value.astype(BF16)
        out_ref[t, :, 256:384] = head
        out_ref[t, :, 384:512] = (value - head.astype(F32)).astype(BF16)


def update_kernel(own_ref, mate_ref, next_ref, far_up_ref, far_down_ref, psf_ref, out_ref, rows_ref, taps_ref, ratio_ref, back_ref):
    def group(ref, g):
        return ref[:, :, g * 128 : g * 128 + 128].astype(F32).reshape(Z, 128)

    even = lax.axis_index("tile") % 2 == 0

    def above(g):
        return jnp.where(even, group(next_ref, g), group(mate_ref, g))

    def below(g):
        return jnp.where(even, group(mate_ref, g), group(next_ref, g))

    blocks = [group(far_up_ref, 0), above(0), above(1), group(own_ref, 0)]
    blocks += [group(own_ref, 1), below(0), below(1), group(far_down_ref, 0)]
    for i, block in enumerate(blocks):
        rows_ref[i * 128 : i * 128 + 128, :] = block.T
    for y in range(H + 4 * R):
        at = S * (y + 2)
        for b in range(E):
            taps_ref[y * W : y * W + W, b * 128 : b * 128 + 128] = rows_ref[at + b : at + b + W, :].astype(BF16)
    rows = H + 2 * R
    total = jnp.zeros((rows * W, Z), F32)
    for a in range(E):
        total = total + jnp.dot(
            taps_ref[a * W : a * W + rows * W, :], psf_ref[a].reshape(E * Z, Z), preferred_element_type=F32
        )

    pitch = 48
    zeros = jnp.zeros((16, 128), F32)
    measured_up = (above(2) + above(3)).T
    measured_own = (group(own_ref, 2) + group(own_ref, 3)).T
    measured_down = (below(2) + below(3)).T
    measured = jnp.concatenate([measured_up[(H - R) * W :], measured_own, measured_down[: R * W]], axis=0)
    ratio = (measured / total).astype(BF16).astype(F32)
    for y in range(rows):
        ratio_ref[y * pitch : y * pitch + 16, :] = zeros
        ratio_ref[y * pitch + 16 : y * pitch + 32, :] = ratio[y * W : y * W + W]
        ratio_ref[y * pitch + 32 : y * pitch + 48, :] = zeros
    last = lax.broadcasted_iota(jnp.int32, (S, 128), 0) == S - 1
    for y in range(rows):
        for b in range(E):
            start = y * pitch + 16 - b
            value = jnp.where(last, 1.0, ratio_ref[start : start + S, :])
            back_ref[y * S : y * S + S, b * 128 : b * 128 + 128] = value.astype(BF16)
    total = jnp.zeros((Z, H * S), F32)
    for a in range(E):
        kernel = jnp.concatenate([psf_ref[a, b] for b in range(E)], axis=1)
        start = (2 * R - a) * S
        total = total + lax.dot_general(
            kernel, back_ref[start : start + H * S, :], (((1,), (1,)), ((), ())), preferred_element_type=F32
        )
    out_ref[...] = total.reshape(TILES, 8, H * S)


def final_kernel(parts_ref, vol_ref, out_ref):
    lane = lanes()
    weight = parts_ref[0, :, S - 1 : S]

    for y in range(H):
        g, s = y // 4, y % 4
        turned = []
        for t in range(TILES):
            part = parts_ref[t, :, g * 128 : g * 128 + 128]
            shift = (W * t - R - S * s) % 128
            turned.append(pltpu.roll(part, shift, 1) if shift else part)
        for half in range(2):
            sums = [None, None]
            for t in range(TILES):
                start, stop = W * t - R - 128 * half, W * t + W + R - 128 * half
                start, stop = max(start, 0), min(stop, 128)
                if start >= stop:
                    continue
                before = sums[t % 2]
                sums[t % 2] = jnp.where(
                    (lane >= start) & (lane < stop), turned[t], 0.0 if before is None else before
                )
            here = slice(half * 128, half * 128 + 128)
            out_ref[:, y, here] = vol_ref[:, y, here] * (sums[0] + sums[1]) / weight


def neighbours(x):
    count = lax.axis_size("tile")
    chips = [(i, i + 1) for i in range(1, count - 1, 2)] + [(i, i - 1) for i in range(2, count, 2)]
    cores = [(i, i + 1) for i in range(0, count, 2)] + [(i, i - 1) for i in range(1, count, 2)]
    mate = lax.ppermute(x, "tile", cores)
    far_down = lax.ppermute(x[:, :, :128], "tile", [(i + 2, i) for i in range(count - 2)])
    far_up = lax.ppermute(x[:, :, 128:256], "tile", [(i, i + 2) for i in range(count - 2)])
    beyond = lax.ppermute(x, "tile", chips)
    return mate, beyond, far_up, far_down


def body(volume, measured, point_spread):
    packed = pl.pallas_call(
        pack_kernel,
        out_shape=jax.ShapeDtypeStruct((TILES, 8, 512), BF16),
        in_specs=[HBM] * 2,
        out_specs=VM,
        scratch_shapes=[
            pltpu.VMEM(volume.shape, F32),
            pltpu.VMEM(measured.shape, F32),
            pltpu.SemaphoreType.DMA((2,)),
        ],
        compiler_params=pltpu.CompilerParams(vmem_limit_bytes=56 * 1024 * 1024),
        cost_estimate=pl.CostEstimate(flops=20_000_000_000, bytes_accessed=2**20, transcendentals=0),
        name="pack",
    )(volume, measured)
    own = lax.all_to_all(packed, "depth", 0, 0, tiled=True)
    shares = pl.pallas_call(
        update_kernel,
        out_shape=jax.ShapeDtypeStruct((TILES, 8, H * S), F32),
        in_specs=[VM] * 6,
        out_specs=VM,
        scratch_shapes=[
            pltpu.VMEM((8 * 128, 128), F32),
            pltpu.VMEM(((H + 4 * R) * W, E * Z), BF16),
            pltpu.VMEM(((H + 2 * R) * 48, 128), F32),
            pltpu.VMEM(((H + 2 * R) * S, E * Z), BF16),
        ],
        compiler_params=PARAMS,
        name="update",
    )(own, *neighbours(own), point_spread)
    parts = lax.all_to_all(shares, "depth", 0, 0, tiled=True)
    return pl.pallas_call(
        final_kernel,
        out_shape=jax.ShapeDtypeStruct(volume.shape, F32),
        in_specs=[VM, VM],
        out_specs=VM,
        compiler_params=PARAMS,
        name="final",
    )(parts, volume)


def solution(mesh):
    in_specs = (P("depth", "tile", None), P("depth", "tile", None), P())
    out_specs = P("depth", "tile", None)
    return jax.shard_map(body, mesh=mesh, in_specs=in_specs, out_specs=out_specs, check_vma=False)
```

```python
import jax
import jax.numpy as jnp
from jax import lax
from jax.experimental import pallas as pl
from jax.experimental.pallas import tpu as pltpu
from jax.sharding import Mesh
from jax.sharding import PartitionSpec as P

R = 5
E = 11
Z = 128
TILES = 16
W = 16
H = 8
S = 32
F32 = jnp.float32
BF16 = jnp.bfloat16
VM = pl.BlockSpec(memory_space=pltpu.VMEM)
HBM = pl.BlockSpec(memory_space=pl.ANY)
PARAMS = pltpu.CompilerParams(vmem_limit_bytes=40 * 1024 * 1024)


def lanes(shape=(8, 128)):
    return lax.broadcasted_iota(jnp.int32, shape, 1)


def pack_kernel(vol_hbm, meas_hbm, out_ref, vol_ref, meas_ref, sems):
    copies = [
        pltpu.make_async_copy(vol_hbm, vol_ref, sems.at[0]),
        pltpu.make_async_copy(meas_hbm, meas_ref, sems.at[1]),
    ]
    for copy in copies:
        copy.start()
    copies[0].wait()
    lane = lanes()
    slot = lane // S
    inside = lane % S
    rolled = {}

    def turned(ref, key, y, half, shift):
        name = (key, y, half, shift % 128)
        if name not in rolled:
            part = ref[:, y, half * 128 : half * 128 + 128]
            rolled[name] = pltpu.roll(part, shift % 128, 1) if shift % 128 else part
        return rolled[name]

    def window(t, y):
        start = W * t - R
        shift = S * (y % 4) - start
        low, high = max(start, 0) // 128, min(start + W + 2 * R - 1, 255) // 128
        value = turned(vol_ref, 0, y, low, shift)
        if high != low:
            value = jnp.where(inside < 128 - start, value, turned(vol_ref, 0, y, high, shift))
        if start < 0:
            value = jnp.where(inside < -start, 0.0, value)
        if start + W + 2 * R > 256:
            value = jnp.where(inside < 256 - start, value, 0.0)
        return value

    for t in range(TILES):
        for g in range(2):
            value = window(t, 4 * g)
            for s in range(1, 4):
                value = jnp.where(slot < s, value, window(t, 4 * g + s))
            out_ref[t, :, g * 128 : g * 128 + 128] = value.astype(BF16)
    copies[1].wait()
    for t in range(TILES):
        value = turned(meas_ref, 1, 0, t // 8, -W * t)
        for y in range(1, H):
            value = jnp.where(lane < W * y, value, turned(meas_ref, 1, y, t // 8, W * y - W * t))
        head = value.astype(BF16)
        out_ref[t, :, 256:384] = head
        out_ref[t, :, 384:512] = (value - head.astype(F32)).astype(BF16)


def ratio_kernel(own_ref, chip_ref, next_ref, psf_ref, out_ref, rows_ref, taps_ref):
    def group(ref, g):
        return ref[:, :, g * 128 : g * 128 + 128].astype(F32).reshape(Z, 128)

    core = lax.axis_index("core")
    even = core == 0
    mate_ref = chip_ref.at[1 - core]

    def above(g):
        return jnp.where(even, group(next_ref, g), group(mate_ref, g))

    def below(g):
        return jnp.where(even, group(mate_ref, g), group(next_ref, g))

    lane = lanes((Z, 128))
    mixed = jnp.where(lane < S, below(1), above(0))
    blocks = [mixed, above(1), group(own_ref, 0), group(own_ref, 1), below(0)]
    for i, block in enumerate(blocks):
        rows_ref[i * 128 : i * 128 + 128, :] = block.T
    for y in range(H + 2 * R):
        at = S * ((3 + y) % 20)
        for b in range(E):
            taps_ref[y * W : y * W + W, b * 128 : b * 128 + 128] = rows_ref[at + b : at + b + W, :].astype(BF16)
    total = jnp.zeros((H * W, Z), F32)
    for a in range(E):
        total = total + jnp.dot(
            taps_ref[a * W : a * W + H * W, :], psf_ref[a].reshape(E * Z, Z), preferred_element_type=F32
        )
    measured = (group(own_ref, 2) + group(own_ref, 3)).T
    out_ref[...] = (measured / total).astype(BF16)


def back_kernel(own_ref, chip_ref, next_ref, psf_ref, out_ref, rows_ref, sum_ref):
    core = lax.axis_index("core")
    even = core == 0
    mate_ref = chip_ref.at[1 - core]
    for y in range(H + 2 * R):
        if y < R:
            here = slice((y + H - R) * W, (y + H - R) * W + W)
            value = jnp.where(even, next_ref[here, :].astype(F32), mate_ref[here, :].astype(F32)).astype(BF16)
        elif y < R + H:
            value = own_ref[(y - R) * W : (y - R) * W + W, :]
        else:
            here = slice((y - R - H) * W, (y - R - H) * W + W)
            value = jnp.where(even, mate_ref[here, :].astype(F32), next_ref[here, :].astype(F32)).astype(BF16)
        for a in range(E):
            row = y + a - 2 * R
            if 0 <= row < H:
                rows_ref[row * W : row * W + W, a * 128 : a * 128 + 128] = value
    rows_ref[H * W : H * W + W, :] = jnp.ones((W, E * Z), BF16)
    sum_ref[...] = jnp.zeros((H * S, Z), F32)
    weight = jnp.zeros((1, Z), F32)
    for first in range(0, E, 2):
        pair = range(first, min(first + 2, E))
        kernel = jnp.concatenate(
            [psf_ref[a, first : first + len(pair)].reshape(len(pair) * Z, Z) for a in range(E)], axis=1
        )
        product = lax.dot_general(rows_ref[...], kernel, (((1,), (1,)), ((), ())), preferred_element_type=F32)
        for i, b in enumerate(pair):
            part = product[:, i * Z : i * Z + Z]
            for y in range(H):
                here = slice(y * S + b, y * S + b + W)
                sum_ref[here, :] = sum_ref[here, :] + part[y * W : y * W + W]
            weight = weight + part[H * W : H * W + 1]
    sum_ref[S - 1 : S, :] = weight
    for g in range(2):
        out_ref[:, :, g * 128 : g * 128 + 128] = sum_ref[g * 128 : g * 128 + 128, :].T.reshape(TILES, 8, 128)


def final_kernel(parts_ref, vol_ref, out_ref):
    lane = lanes()
    weight = parts_ref[0, :, S - 1 : S]

    for y in range(H):
        g, s = y // 4, y % 4
        turned = []
        for t in range(TILES):
            part = parts_ref[t, :, g * 128 : g * 128 + 128]
            shift = (W * t - R - S * s) % 128
            turned.append(pltpu.roll(part, shift, 1) if shift else part)
        for half in range(2):
            sums = [None, None]
            for t in range(TILES):
                start, stop = W * t - R - 128 * half, W * t + W + R - 128 * half
                start, stop = max(start, 0), min(stop, 128)
                if start >= stop:
                    continue
                before = sums[t % 2]
                sums[t % 2] = jnp.where(
                    (lane >= start) & (lane < stop), turned[t], 0.0 if before is None else before
                )
            here = slice(half * 128, half * 128 + 128)
            out_ref[:, y, here] = vol_ref[:, y, here] * (sums[0] + sums[1]) / weight


def neighbours(x):
    tile = ("pair", "core")
    count = lax.axis_size(tile)
    chips = [(i, i + 1) for i in range(1, count - 1, 2)] + [(i, i - 1) for i in range(2, count, 2)]
    beyond = lax.ppermute(x, tile, chips)
    return lax.all_gather(x, "core"), beyond


def body(volume, measured, point_spread):
    packed = pl.pallas_call(
        pack_kernel,
        out_shape=jax.ShapeDtypeStruct((TILES, 8, 512), BF16),
        in_specs=[HBM] * 2,
        out_specs=VM,
        scratch_shapes=[
            pltpu.VMEM(volume.shape, F32),
            pltpu.VMEM(measured.shape, F32),
            pltpu.SemaphoreType.DMA((2,)),
        ],
        compiler_params=pltpu.CompilerParams(vmem_limit_bytes=56 * 1024 * 1024),
        cost_estimate=pl.CostEstimate(flops=20_000_000_000, bytes_accessed=2**20, transcendentals=0),
        name="pack",
    )(volume, measured)
    own = lax.all_to_all(packed, "depth", 0, 0, tiled=True)
    chip, beyond = neighbours(own[:, :, :256])
    ratio = pl.pallas_call(
        ratio_kernel,
        out_shape=jax.ShapeDtypeStruct((H * W, Z), BF16),
        in_specs=[VM] * 4,
        out_specs=VM,
        scratch_shapes=[
            pltpu.VMEM((5 * 128, 128), F32),
            pltpu.VMEM(((H + 2 * R) * W, E * Z), BF16),
        ],
        compiler_params=PARAMS,
        name="ratio",
    )(own, chip, beyond, point_spread)
    chip, beyond = neighbours(ratio)
    shares = pl.pallas_call(
        back_kernel,
        out_shape=jax.ShapeDtypeStruct((TILES, 8, H * S), F32),
        in_specs=[VM] * 4,
        out_specs=VM,
        scratch_shapes=[
            pltpu.VMEM((H * W + W, E * Z), BF16),
            pltpu.VMEM((H * S, Z), F32),
        ],
        compiler_params=PARAMS,
        name="back",
    )(ratio, chip, beyond, point_spread)
    parts = lax.all_to_all(shares, "depth", 0, 0, tiled=True)
    return pl.pallas_call(
        final_kernel,
        out_shape=jax.ShapeDtypeStruct(volume.shape, F32),
        in_specs=[VM, VM],
        out_specs=VM,
        compiler_params=PARAMS,
        name="final",
    )(parts, volume)


def solution(mesh):
    depth, tile = mesh.devices.shape
    split = Mesh(mesh.devices.reshape(depth, tile // 2, 2), ("depth", "pair", "core"))
    spec = P("depth", ("pair", "core"), None)
    return jax.shard_map(body, mesh=split, in_specs=(spec, spec, P()), out_specs=spec, check_vma=False)
```

```python
import jax
import jax.numpy as jnp
from jax import lax
from jax.experimental import pallas as pl
from jax.experimental.pallas import tpu as pltpu
from jax.sharding import Mesh
from jax.sharding import PartitionSpec as P

R = 5
E = 11
Z = 128
TILES = 16
W = 16
H = 8
S = 32
CHUNKS = ((0, 13),)
F32 = jnp.float32
BF16 = jnp.bfloat16
VM = pl.BlockSpec(memory_space=pltpu.VMEM)
HBM = pl.BlockSpec(memory_space=pl.ANY)
PARAMS = pltpu.CompilerParams(vmem_limit_bytes=40 * 1024 * 1024)


def lanes(shape=(8, 128)):
    return lax.broadcasted_iota(jnp.int32, shape, 1)


def pack_kernel(vol_hbm, meas_hbm, out_ref, vol_ref, meas_ref, sems):
    copies = [
        pltpu.make_async_copy(vol_hbm, vol_ref, sems.at[0]),
        pltpu.make_async_copy(meas_hbm, meas_ref, sems.at[1]),
    ]
    for copy in copies:
        copy.start()
    copies[0].wait()
    lane = lanes()
    slot = lane // S
    inside = lane % S
    rolled = {}

    def turned(ref, key, y, half, shift):
        name = (key, y, half, shift % 128)
        if name not in rolled:
            part = ref[:, y, half * 128 : half * 128 + 128]
            rolled[name] = pltpu.roll(part, shift % 128, 1) if shift % 128 else part
        return rolled[name]

    def window(t, y):
        start = W * t - R
        shift = S * (y % 4) - start
        low, high = max(start, 0) // 128, min(start + W + 2 * R - 1, 255) // 128
        value = turned(vol_ref, 0, y, low, shift)
        if high != low:
            value = jnp.where(inside < 128 - start, value, turned(vol_ref, 0, y, high, shift))
        if start < 0:
            value = jnp.where(inside < -start, 0.0, value)
        if start + W + 2 * R > 256:
            value = jnp.where(inside < 256 - start, value, 0.0)
        return value

    for t in range(TILES):
        for g in range(2):
            value = window(t, 4 * g)
            for s in range(1, 4):
                value = jnp.where(slot < s, value, window(t, 4 * g + s))
            out_ref[t, :, g * 128 : g * 128 + 128] = value.astype(BF16)
    copies[1].wait()
    for t in range(TILES):
        value = turned(meas_ref, 1, 0, t // 8, -W * t)
        for y in range(1, H):
            value = jnp.where(lane < W * y, value, turned(meas_ref, 1, y, t // 8, W * y - W * t))
        head = value.astype(BF16)
        out_ref[t, :, 256:384] = head
        out_ref[t, :, 384:512] = (value - head.astype(F32)).astype(BF16)


def join_kernel(own_ref, chip_ref, out_ref):
    even = lax.axis_index("core") == 0
    out_ref[:, :, :512] = own_ref[...]
    upper, lower = chip_ref[1, :, :, :128], chip_ref[0, :, :, 128:]
    out_ref[:, :, 512:] = jnp.where(even, upper.astype(F32), lower.astype(F32)).astype(BF16)


def ratio_kernel(own_ref, chip_ref, next_ref, psf_ref, out_ref, rows_ref, taps_ref, meas_ref):
    core = lax.axis_index("core")
    even = core == 0

    def group(value, g):
        return value[:, :, g * 128 : g * 128 + 128].astype(F32).reshape(Z, 128)

    upper, lower = chip_ref[0], chip_ref[1]
    chip = [group(upper, 0), group(upper, 1), group(lower, 0), group(lower, 1)]
    beyond = [group(next_ref, 0), group(next_ref, 1), group(next_ref, 4)]
    when_even = [beyond[2], beyond[0], beyond[1], *chip]
    when_odd = [*chip, *beyond]
    shift = S * (1 - core)
    for i, (a, b) in enumerate(zip(when_even, when_odd)):
        rows_ref[pl.ds(pl.multiple_of(i * 128 + shift, S), 128), :] = jnp.where(even, a, b).T
    rows = H + R
    for y in range(rows + 2 * R):
        at = S * (y + 3)
        for b in range(E):
            taps_ref[y * W : y * W + W, b * 128 : b * 128 + 128] = rows_ref[at + b : at + b + W, :].astype(BF16)
    here = (group(own_ref, 2) + group(own_ref, 3)).T
    there = (group(next_ref, 2) + group(next_ref, 3)).T
    skip = (H - R) * W
    meas_ref[pl.ds(pl.multiple_of(jnp.where(even, H * W, skip), 16), H * W), :] = here
    meas_ref[pl.ds(pl.multiple_of(jnp.where(even, 0, skip + H * W), 16), H * W), :] = there
    for first, count in CHUNKS:
        total = jnp.zeros((count * W, Z), F32)
        for a in range(E):
            total = total + jnp.dot(
                taps_ref[(first + a) * W : (first + a + count) * W, :],
                psf_ref[a].reshape(E * Z, Z),
                preferred_element_type=F32,
            )
        part = slice(first * W, (first + count) * W)
        out_ref[part, :] = (meas_ref[skip + first * W : skip + (first + count) * W, :] / total).astype(BF16)


def back_kernel(chip_ref, psf_ref, out_ref, rows_ref, sum_ref):
    first_row = lax.axis_index("core") * (H * W)
    for y in range(H + 2 * R):
        value = chip_ref[pl.ds(pl.multiple_of(first_row + y * W, W), W), :]
        for a in range(E):
            row = y + a - 2 * R
            if 0 <= row < H:
                rows_ref[row * W : row * W + W, a * 128 : a * 128 + 128] = value
    rows_ref[H * W : H * W + W, :] = jnp.ones((W, E * Z), BF16)
    sum_ref[...] = jnp.zeros((H * S, Z), F32)
    weight = jnp.zeros((1, Z), F32)
    for first in range(0, E, 2):
        pair = range(first, min(first + 2, E))
        kernel = jnp.concatenate(
            [psf_ref[a, first : first + len(pair)].reshape(len(pair) * Z, Z) for a in range(E)], axis=1
        )
        product = lax.dot_general(rows_ref[...], kernel, (((1,), (1,)), ((), ())), preferred_element_type=F32)
        for i, b in enumerate(pair):
            part = product[:, i * Z : i * Z + Z]
            for y in range(H):
                here = slice(y * S + b, y * S + b + W)
                sum_ref[here, :] = sum_ref[here, :] + part[y * W : y * W + W]
            weight = weight + part[H * W : H * W + 1]
    sum_ref[S - 1 : S, :] = weight
    for g in range(2):
        out_ref[:, :, g * 128 : g * 128 + 128] = sum_ref[g * 128 : g * 128 + 128, :].T.reshape(TILES, 8, 128)


def final_kernel(parts_ref, vol_ref, out_ref):
    lane = lanes()
    weight = parts_ref[0, :, S - 1 : S]

    for y in range(H):
        g, s = y // 4, y % 4
        turned = []
        for t in range(TILES):
            part = parts_ref[t, :, g * 128 : g * 128 + 128]
            shift = (W * t - R - S * s) % 128
            turned.append(pltpu.roll(part, shift, 1) if shift else part)
        for half in range(2):
            sums = [None, None]
            for t in range(TILES):
                start, stop = W * t - R - 128 * half, W * t + W + R - 128 * half
                start, stop = max(start, 0), min(stop, 128)
                if start >= stop:
                    continue
                before = sums[t % 2]
                sums[t % 2] = jnp.where(
                    (lane >= start) & (lane < stop), turned[t], 0.0 if before is None else before
                )
            here = slice(half * 128, half * 128 + 128)
            out_ref[:, y, here] = vol_ref[:, y, here] * (sums[0] + sums[1]) / weight


def body(volume, measured, point_spread):
    packed = pl.pallas_call(
        pack_kernel,
        out_shape=jax.ShapeDtypeStruct((TILES, 8, 512), BF16),
        in_specs=[HBM] * 2,
        out_specs=VM,
        scratch_shapes=[
            pltpu.VMEM(volume.shape, F32),
            pltpu.VMEM(measured.shape, F32),
            pltpu.SemaphoreType.DMA((2,)),
        ],
        compiler_params=pltpu.CompilerParams(vmem_limit_bytes=56 * 1024 * 1024),
        cost_estimate=pl.CostEstimate(flops=20_000_000_000, bytes_accessed=2**20, transcendentals=0),
        name="pack",
    )(volume, measured)
    own = lax.all_to_all(packed, "depth", 0, 0, tiled=True)
    chip = lax.all_gather(own[:, :, :256], "core")
    joined = pl.pallas_call(
        join_kernel,
        out_shape=jax.ShapeDtypeStruct((TILES, 8, 640), BF16),
        in_specs=[VM] * 2,
        out_specs=VM,
        compiler_params=PARAMS,
        name="join",
    )(own, chip)
    tile = ("pair", "core")
    count = lax.axis_size(tile)
    pairs = [(i, i + 1) for i in range(1, count - 1, 2)] + [(i, i - 1) for i in range(2, count, 2)]
    beyond = lax.ppermute(joined, tile, pairs)
    ratio = pl.pallas_call(
        ratio_kernel,
        out_shape=jax.ShapeDtypeStruct(((H + R) * W, Z), BF16),
        in_specs=[VM] * 4,
        out_specs=VM,
        scratch_shapes=[
            pltpu.VMEM((7 * 128 + S, 128), F32),
            pltpu.VMEM(((H + 3 * R) * W, E * Z), BF16),
            pltpu.VMEM((2 * H * W + (H - R) * W, Z), F32),
        ],
        compiler_params=PARAMS,
        name="ratio",
    )(own, chip, beyond, point_spread)
    chip_ratio = lax.all_gather(ratio, "core", tiled=True)
    shares = pl.pallas_call(
        back_kernel,
        out_shape=jax.ShapeDtypeStruct((TILES, 8, H * S), F32),
        in_specs=[VM] * 2,
        out_specs=VM,
        scratch_shapes=[
            pltpu.VMEM((H * W + W, E * Z), BF16),
            pltpu.VMEM((H * S, Z), F32),
        ],
        compiler_params=PARAMS,
        name="back",
    )(chip_ratio, point_spread)
    parts = lax.all_to_all(shares, "depth", 0, 0, tiled=True)
    return pl.pallas_call(
        final_kernel,
        out_shape=jax.ShapeDtypeStruct(volume.shape, F32),
        in_specs=[VM, VM],
        out_specs=VM,
        compiler_params=PARAMS,
        name="final",
    )(parts, volume)


def solution(mesh):
    depth, tile = mesh.devices.shape
    split = Mesh(mesh.devices.reshape(depth, tile // 2, 2), ("depth", "pair", "core"))
    spec = P("depth", ("pair", "core"), None)
    return jax.shard_map(body, mesh=split, in_specs=(spec, spec, P()), out_specs=spec, check_vma=False)
```

```python
import jax
import jax.numpy as jnp
from jax import lax
from jax.experimental import pallas as pl
from jax.experimental.pallas import tpu as pltpu
from jax.sharding import Mesh
from jax.sharding import PartitionSpec as P

R = 5
E = 11
Z = 128
TILES = 16
W = 16
H = 8
S = 32
F32 = jnp.float32
BF16 = jnp.bfloat16
VM = pl.BlockSpec(memory_space=pltpu.VMEM)
PARAMS = pltpu.CompilerParams(vmem_limit_bytes=40 * 1024 * 1024)


def lanes(shape=(8, 128)):
    return lax.broadcasted_iota(jnp.int32, shape, 1)


def pack_kernel(both_ref, out_ref):
    vol_ref, meas_ref = both_ref.at[0], both_ref.at[1]
    lane = lanes()
    slot = lane // S
    inside = lane % S
    rolled = {}

    def turned(ref, key, y, half, shift):
        name = (key, y, half, shift % 128)
        if name not in rolled:
            part = ref[:, y, half * 128 : half * 128 + 128]
            rolled[name] = pltpu.roll(part, shift % 128, 1) if shift % 128 else part
        return rolled[name]

    def window(t, y):
        start = W * t - R
        shift = S * (y % 4) - start
        low, high = max(start, 0) // 128, min(start + W + 2 * R - 1, 255) // 128
        value = turned(vol_ref, 0, y, low, shift)
        if high != low:
            value = jnp.where(inside < 128 - start, value, turned(vol_ref, 0, y, high, shift))
        if start < 0:
            value = jnp.where(inside < -start, 0.0, value)
        if start + W + 2 * R > 256:
            value = jnp.where(inside < 256 - start, value, 0.0)
        return value

    for t in range(TILES):
        for g in range(2):
            value = window(t, 4 * g)
            for s in range(1, 4):
                value = jnp.where(slot < s, value, window(t, 4 * g + s))
            out_ref[t, :, g * 128 : g * 128 + 128] = value.astype(BF16)
    for t in range(TILES):
        value = turned(meas_ref, 1, 0, t // 8, -W * t)
        for y in range(1, H):
            value = jnp.where(lane < W * y, value, turned(meas_ref, 1, y, t // 8, W * y - W * t))
        head = value.astype(BF16)
        out_ref[t, :, 256:384] = head
        out_ref[t, :, 384:512] = (value - head.astype(F32)).astype(BF16)


def group(value, g):
    return value[:, :, g * 128 : g * 128 + 128].astype(F32).reshape(Z, 128)


def join_kernel(own_ref, chip_ref, out_ref):
    core = lax.axis_index("core")
    even = core == 0
    lane = lanes((Z, 128))
    keep = (lane >= 48 * core) & (lane < 80 + 48 * core)
    mate = jnp.where(even, group(chip_ref[1], 0), group(chip_ref[0], 1))
    half = pltpu.roll(mate, 64, 1)
    one = jnp.where(even, pltpu.roll(mate, 96, 1), half)
    two = jnp.where(even, half, pltpu.roll(mate, 32, 1))
    out_ref[:, :, :256] = own_ref[:, :, :256]
    out_ref[:, :, 256:384] = jnp.where(keep, group(own_ref, 2), one).astype(BF16).reshape(TILES, 8, 128)
    out_ref[:, :, 384:] = jnp.where(keep, group(own_ref, 3), two).astype(BF16).reshape(TILES, 8, 128)


def spread_rows(rows_ref, taps_ref, count):
    for y in range(count):
        for b in range(E):
            start = y * S + b
            taps_ref[y * W : y * W + W, b * 128 : b * 128 + 128] = rows_ref[start : start + W, :].astype(BF16)


def add_products(taps_ref, psf_ref, sum_ref, offset, count, taps_row, sum_row):
    part = jnp.dot(
        taps_ref[pl.ds(pl.multiple_of(taps_row * W, W), count * W), :],
        psf_ref[offset].reshape(E * Z, Z),
        preferred_element_type=F32,
    )
    here = pl.ds(pl.multiple_of(sum_row * W, W), count * W)
    sum_ref[here, :] = sum_ref[here, :] + part


def inner_kernel(own_ref, chip_ref, psf_ref, sum_ref, meas_ref, rows_ref, taps_ref):
    core = lax.axis_index("core")
    for i in range(4):
        rows_ref[i * 128 : i * 128 + 128, :] = group(chip_ref[i // 2], i % 2).T
    meas_ref[...] = (group(own_ref, 2) + group(own_ref, 3)).T
    spread_rows(rows_ref, taps_ref, 2 * H)
    sum_ref[...] = jnp.zeros(sum_ref.shape, F32)
    for k in range(-R, R + 1):
        count = H + k
        add_products(
            taps_ref, psf_ref, sum_ref, R + k * (1 - 2 * core), count, (2 * H - count) * core, (H + R - count) * (1 - core)
        )


def ratio_kernel(inner_ref, meas_ref, next_ref, psf_ref, out_ref, rows_ref, taps_ref, sum_ref):
    core = lax.axis_index("core")
    even = core == 0
    first, second = group(next_ref, 2).T, group(next_ref, 3).T
    shift = 2 * S * (1 - core)
    for g in range(2):
        rows_ref[pl.ds(pl.multiple_of(g * 128 + shift, S), 128), :] = group(next_ref, g).T
    for i, block in enumerate((first, second)):
        at = pl.multiple_of(i * S + 8 * S * core, S)
        rows_ref[pl.ds(at, S), :] = jnp.where(even, block[:S], block[128 - S :])
    spread_rows(rows_ref, taps_ref, 2 * R)
    sum_ref[...] = inner_ref[...]
    for k in range(-R, R):
        count = R - k
        add_products(
            taps_ref, psf_ref, sum_ref, R + k * (1 - 2 * core), count, (2 * R - count) * (1 - core), (H + R - count) * core
        )
    here = pl.ds(pl.multiple_of(R * W * (1 - core), W), H * W)
    out_ref[here, :] = (meas_ref[...] / sum_ref[here, :]).astype(BF16)
    there = pl.ds(pl.multiple_of(H * W * core, W), R * W)
    beyond = first + second
    beyond = jnp.where(even, beyond[(H - R) * W :], beyond[: R * W])
    out_ref[there, :] = (beyond / sum_ref[there, :]).astype(BF16)


def back_kernel(chip_ref, psf_ref, out_ref, rows_ref, sum_ref):
    first_row = lax.axis_index("core") * (H * W)
    for y in range(H + 2 * R):
        value = chip_ref[pl.ds(pl.multiple_of(first_row + y * W, W), W), :]
        for a in range(E):
            row = y + a - 2 * R
            if 0 <= row < H:
                rows_ref[row * W : row * W + W, a * 128 : a * 128 + 128] = value
    rows_ref[H * W : H * W + W, :] = jnp.ones((W, E * Z), BF16)
    sum_ref[...] = jnp.zeros((H * S, Z), F32)
    weight = jnp.zeros((1, Z), F32)
    for first in range(0, E, 2):
        pair = range(first, min(first + 2, E))
        kernel = jnp.concatenate(
            [psf_ref[a, first : first + len(pair)].reshape(len(pair) * Z, Z) for a in range(E)], axis=1
        )
        product = lax.dot_general(rows_ref[...], kernel, (((1,), (1,)), ((), ())), preferred_element_type=F32)
        for i, b in enumerate(pair):
            part = product[:, i * Z : i * Z + Z]
            for y in range(H):
                here = slice(y * S + b, y * S + b + W)
                sum_ref[here, :] = sum_ref[here, :] + part[y * W : y * W + W]
            weight = weight + part[H * W : H * W + 1]
    sum_ref[S - 1 : S, :] = weight
    for g in range(2):
        out_ref[:, :, g * 128 : g * 128 + 128] = sum_ref[g * 128 : g * 128 + 128, :].T.reshape(TILES, 8, 128)


def final_kernel(parts_ref, vol_ref, out_ref):
    lane = lanes()
    weight = parts_ref[0, :, S - 1 : S]

    for y in range(H):
        g, s = y // 4, y % 4
        turned = []
        for t in range(TILES):
            part = parts_ref[t, :, g * 128 : g * 128 + 128]
            shift = (W * t - R - S * s) % 128
            turned.append(pltpu.roll(part, shift, 1) if shift else part)
        for half in range(2):
            sums = [None, None]
            for t in range(TILES):
                start, stop = W * t - R - 128 * half, W * t + W + R - 128 * half
                start, stop = max(start, 0), min(stop, 128)
                if start >= stop:
                    continue
                before = sums[t % 2]
                sums[t % 2] = jnp.where(
                    (lane >= start) & (lane < stop), turned[t], 0.0 if before is None else before
                )
            here = slice(half * 128, half * 128 + 128)
            out_ref[:, y, here] = vol_ref[:, y, here] * (sums[0] + sums[1]) / weight


def body(volume, measured, point_spread):
    packed = pl.pallas_call(
        pack_kernel,
        out_shape=jax.ShapeDtypeStruct((TILES, 8, 512), BF16),
        in_specs=[VM],
        out_specs=VM,
        compiler_params=PARAMS,
        cost_estimate=pl.CostEstimate(flops=20_000_000_000, bytes_accessed=2**20, transcendentals=0),
        name="pack",
    )(jnp.stack([volume, measured]))
    own = lax.all_to_all(packed, "depth", 0, 0, tiled=True)
    chip = lax.all_gather(own[:, :, :256], "core")
    joined = pl.pallas_call(
        join_kernel,
        out_shape=jax.ShapeDtypeStruct((TILES, 8, 512), BF16),
        in_specs=[VM] * 2,
        out_specs=VM,
        compiler_params=PARAMS,
        name="join",
    )(own, chip)
    tile = ("pair", "core")
    count = lax.axis_size(tile)
    pairs = [(i, i + 1) for i in range(1, count - 1, 2)] + [(i, i - 1) for i in range(2, count, 2)]
    beyond = lax.ppermute(joined, tile, pairs)
    rows = H + R
    inner, near = pl.pallas_call(
        inner_kernel,
        out_shape=[jax.ShapeDtypeStruct((rows * W, Z), F32), jax.ShapeDtypeStruct((H * W, Z), F32)],
        in_specs=[VM] * 3,
        out_specs=[VM] * 2,
        scratch_shapes=[
            pltpu.VMEM((2 * H * S, Z), F32),
            pltpu.VMEM((2 * H * W, E * Z), BF16),
        ],
        compiler_params=PARAMS,
        cost_estimate=pl.CostEstimate(flops=2 * 88 * W * E * Z * Z, bytes_accessed=2**22, transcendentals=0),
        name="inner",
    )(own, chip, point_spread)
    ratio = pl.pallas_call(
        ratio_kernel,
        out_shape=jax.ShapeDtypeStruct((rows * W, Z), BF16),
        in_specs=[VM] * 4,
        out_specs=VM,
        scratch_shapes=[
            pltpu.VMEM((2 * R * S, Z), F32),
            pltpu.VMEM((2 * R * W, E * Z), BF16),
            pltpu.VMEM((rows * W, Z), F32),
        ],
        compiler_params=PARAMS,
        name="ratio",
    )(inner, near, beyond, point_spread)
    chip_ratio = lax.all_gather(ratio, "core", tiled=True)
    shares = pl.pallas_call(
        back_kernel,
        out_shape=jax.ShapeDtypeStruct((TILES, 8, H * S), F32),
        in_specs=[VM] * 2,
        out_specs=VM,
        scratch_shapes=[
            pltpu.VMEM((H * W + W, E * Z), BF16),
            pltpu.VMEM((H * S, Z), F32),
        ],
        compiler_params=PARAMS,
        name="back",
    )(chip_ratio, point_spread)
    parts = lax.all_to_all(shares, "depth", 0, 0, tiled=True)
    return pl.pallas_call(
        final_kernel,
        out_shape=jax.ShapeDtypeStruct(volume.shape, F32),
        in_specs=[VM, VM],
        out_specs=VM,
        compiler_params=PARAMS,
        name="final",
    )(parts, volume)


def solution(mesh):
    depth, tile = mesh.devices.shape
    split = Mesh(mesh.devices.reshape(depth, tile // 2, 2), ("depth", "pair", "core"))
    spec = P("depth", ("pair", "core"), None)
    return jax.shard_map(body, mesh=split, in_specs=(spec, spec, P()), out_specs=spec, check_vma=False)
```

```python
import jax
import jax.numpy as jnp
from jax import lax
from jax.experimental import pallas as pl
from jax.experimental.pallas import tpu as pltpu
from jax.sharding import Mesh
from jax.sharding import PartitionSpec as P

R = 5
E = 11
Z = 128
TILES = 16
W = 16
H = 8
S = 32
F32 = jnp.float32
BF16 = jnp.bfloat16
VM = pl.BlockSpec(memory_space=pltpu.VMEM)
PARAMS = pltpu.CompilerParams(vmem_limit_bytes=40 * 1024 * 1024)


def lanes(shape=(8, 128)):
    return lax.broadcasted_iota(jnp.int32, shape, 1)


def pack_kernel(vol_ref, meas_ref, out_ref):
    lane = lanes()
    slot = lane // S
    inside = lane % S
    rolled = {}

    def turned(ref, key, y, half, shift):
        name = (key, y, half, shift % 128)
        if name not in rolled:
            part = ref[*key, :, y, half * 128 : half * 128 + 128]
            rolled[name] = pltpu.roll(part, shift % 128, 1) if shift % 128 else part
        return rolled[name]

    def window(t, y):
        start = W * t - R
        shift = S * (y % 4) - start
        low, high = max(start, 0) // 128, min(start + W + 2 * R - 1, 255) // 128
        tile, y = (y // H,), y % H
        value = turned(vol_ref, tile, y, low, shift)
        if high != low:
            value = jnp.where(inside < 128 - start, value, turned(vol_ref, tile, y, high, shift))
        if start < 0:
            value = jnp.where(inside < -start, 0.0, value)
        if start + W + 2 * R > 256:
            value = jnp.where(inside < 256 - start, value, 0.0)
        return value

    for t in range(TILES):
        for g in range(4):
            value = window(t, 4 * g)
            for s in range(1, 4):
                value = jnp.where(slot < s, value, window(t, 4 * g + s))
            out_ref[t, :, g * 128 : g * 128 + 128] = value.astype(BF16)
    for t in range(TILES):
        value = turned(meas_ref, (), 0, t // 8, -W * t)
        for y in range(1, H):
            value = jnp.where(lane < W * y, value, turned(meas_ref, (), y, t // 8, W * y - W * t))
        head = value.astype(BF16)
        out_ref[t, :, 512:640] = head
        out_ref[t, :, 640:768] = (value - head.astype(F32)).astype(BF16)


def group(value, g):
    return value[:, :, g * 128 : g * 128 + 128].astype(F32).reshape(Z, 128)


def join_kernel(own_ref, out_ref):
    core = lax.axis_index("core")
    even = core == 0
    lane = lanes((Z, 128))
    keep = (lane >= 48 * core) & (lane < 80 + 48 * core)
    upper, lower = [[group(own_ref, 2 * i + g) for g in range(2)] for i in range(2)]
    mate = jnp.where(even, lower[0], upper[1])
    half = pltpu.roll(mate, 64, 1)
    one = jnp.where(even, pltpu.roll(mate, 96, 1), half)
    two = jnp.where(even, half, pltpu.roll(mate, 32, 1))
    parts = [jnp.where(even, upper[g], lower[g]) for g in range(2)]
    parts += [jnp.where(keep, group(own_ref, 4), one), jnp.where(keep, group(own_ref, 5), two)]
    for g, part in enumerate(parts):
        out_ref[:, :, g * 128 : g * 128 + 128] = part.astype(BF16).reshape(TILES, 8, 128)


def spread_rows(rows_ref, taps_ref, count):
    for y in range(count):
        for b in range(E):
            start = y * S + b
            taps_ref[y * W : y * W + W, b * 128 : b * 128 + 128] = rows_ref[start : start + W, :].astype(BF16)


def add_products(taps_ref, psf_ref, sum_ref, offset, count, taps_row, sum_row):
    part = jnp.dot(
        taps_ref[pl.ds(pl.multiple_of(taps_row * W, W), count * W), :],
        psf_ref[offset].reshape(E * Z, Z),
        preferred_element_type=F32,
    )
    here = pl.ds(pl.multiple_of(sum_row * W, W), count * W)
    sum_ref[here, :] = sum_ref[here, :] + part


def inner_kernel(own_ref, psf_ref, sum_ref, meas_ref, rows_ref, taps_ref):
    core = lax.axis_index("core")
    for i in range(4):
        rows_ref[i * 128 : i * 128 + 128, :] = group(own_ref, i).T
    meas_ref[...] = (group(own_ref, 4) + group(own_ref, 5)).T
    spread_rows(rows_ref, taps_ref, 2 * H)
    sum_ref[...] = jnp.zeros(sum_ref.shape, F32)
    for k in range(-R, R + 1):
        count = H + k
        add_products(
            taps_ref, psf_ref, sum_ref, R + k * (1 - 2 * core), count, (2 * H - count) * core, (H + R - count) * (1 - core)
        )


def ratio_kernel(inner_ref, meas_ref, next_ref, psf_ref, out_ref, rows_ref, taps_ref, sum_ref):
    core = lax.axis_index("core")
    even = core == 0
    first, second = group(next_ref, 2).T, group(next_ref, 3).T
    shift = 2 * S * (1 - core)
    for g in range(2):
        rows_ref[pl.ds(pl.multiple_of(g * 128 + shift, S), 128), :] = group(next_ref, g).T
    for i, block in enumerate((first, second)):
        at = pl.multiple_of(i * S + 8 * S * core, S)
        rows_ref[pl.ds(at, S), :] = jnp.where(even, block[:S], block[128 - S :])
    spread_rows(rows_ref, taps_ref, 2 * R)
    sum_ref[...] = inner_ref[...]
    for k in range(-R, R):
        count = R - k
        add_products(
            taps_ref, psf_ref, sum_ref, R + k * (1 - 2 * core), count, (2 * R - count) * (1 - core), (H + R - count) * core
        )
    here = pl.ds(pl.multiple_of(R * W * (1 - core), W), H * W)
    out_ref[here, :] = (meas_ref[...] / sum_ref[here, :]).astype(BF16)
    there = pl.ds(pl.multiple_of(H * W * core, W), R * W)
    beyond = first + second
    beyond = jnp.where(even, beyond[(H - R) * W :], beyond[: R * W])
    out_ref[there, :] = (beyond / sum_ref[there, :]).astype(BF16)


def back_kernel(chip_ref, psf_ref, out_ref, rows_ref, sum_ref):
    first_row = lax.axis_index("core") * (H * W)
    for y in range(H + 2 * R):
        value = chip_ref[pl.ds(pl.multiple_of(first_row + y * W, W), W), :]
        for a in range(E):
            row = y + a - 2 * R
            if 0 <= row < H:
                rows_ref[row * W : row * W + W, a * 128 : a * 128 + 128] = value
    rows_ref[H * W : H * W + W, :] = jnp.ones((W, E * Z), BF16)
    sum_ref[...] = jnp.zeros((H * S, Z), F32)
    weight = jnp.zeros((1, Z), F32)
    for first in range(0, E, 2):
        pair = range(first, min(first + 2, E))
        kernel = jnp.concatenate(
            [psf_ref[a, first : first + len(pair)].reshape(len(pair) * Z, Z) for a in range(E)], axis=1
        )
        product = lax.dot_general(rows_ref[...], kernel, (((1,), (1,)), ((), ())), preferred_element_type=F32)
        for i, b in enumerate(pair):
            part = product[:, i * Z : i * Z + Z]
            for y in range(H):
                here = slice(y * S + b, y * S + b + W)
                sum_ref[here, :] = sum_ref[here, :] + part[y * W : y * W + W]
            weight = weight + part[H * W : H * W + 1]
    sum_ref[S - 1 : S, :] = weight
    for g in range(2):
        out_ref[:, :, g * 128 : g * 128 + 128] = sum_ref[g * 128 : g * 128 + 128, :].T.reshape(TILES, 8, 128)


def final_kernel(parts_ref, vol_ref, out_ref):
    lane = lanes()
    weight = parts_ref[0, :, S - 1 : S]

    for y in range(H):
        g, s = y // 4, y % 4
        turned = []
        for t in range(TILES):
            part = parts_ref[t, :, g * 128 : g * 128 + 128]
            shift = (W * t - R - S * s) % 128
            turned.append(pltpu.roll(part, shift, 1) if shift else part)
        for half in range(2):
            sums = [None, None]
            for t in range(TILES):
                start, stop = W * t - R - 128 * half, W * t + W + R - 128 * half
                start, stop = max(start, 0), min(stop, 128)
                if start >= stop:
                    continue
                before = sums[t % 2]
                sums[t % 2] = jnp.where(
                    (lane >= start) & (lane < stop), turned[t], 0.0 if before is None else before
                )
            here = slice(half * 128, half * 128 + 128)
            out_ref[:, y, here] = vol_ref[:, y, here] * (sums[0] + sums[1]) / weight


def body(volume, measured, point_spread):
    packed = pl.pallas_call(
        pack_kernel,
        out_shape=jax.ShapeDtypeStruct((TILES, 8, 768), BF16),
        in_specs=[VM] * 2,
        out_specs=VM,
        compiler_params=PARAMS,
        cost_estimate=pl.CostEstimate(flops=20_000_000_000, bytes_accessed=2**20, transcendentals=0),
        name="pack",
    )(lax.all_gather(volume, "core"), measured)
    own = lax.all_to_all(packed, "depth", 0, 0, tiled=True)
    joined = pl.pallas_call(
        join_kernel,
        out_shape=jax.ShapeDtypeStruct((TILES, 8, 512), BF16),
        in_specs=[VM],
        out_specs=VM,
        compiler_params=PARAMS,
        name="join",
    )(own)
    tile = ("pair", "core")
    count = lax.axis_size(tile)
    pairs = [(i, i + 1) for i in range(1, count - 1, 2)] + [(i, i - 1) for i in range(2, count, 2)]
    beyond = lax.ppermute(joined, tile, pairs)
    rows = H + R
    inner, near = pl.pallas_call(
        inner_kernel,
        out_shape=[jax.ShapeDtypeStruct((rows * W, Z), F32), jax.ShapeDtypeStruct((H * W, Z), F32)],
        in_specs=[VM] * 2,
        out_specs=[VM] * 2,
        scratch_shapes=[
            pltpu.VMEM((2 * H * S, Z), F32),
            pltpu.VMEM((2 * H * W, E * Z), BF16),
        ],
        compiler_params=PARAMS,
        cost_estimate=pl.CostEstimate(flops=2 * 88 * W * E * Z * Z, bytes_accessed=2**22, transcendentals=0),
        name="inner",
    )(own, point_spread)
    ratio = pl.pallas_call(
        ratio_kernel,
        out_shape=jax.ShapeDtypeStruct((rows * W, Z), BF16),
        in_specs=[VM] * 4,
        out_specs=VM,
        scratch_shapes=[
            pltpu.VMEM((2 * R * S, Z), F32),
            pltpu.VMEM((2 * R * W, E * Z), BF16),
            pltpu.VMEM((rows * W, Z), F32),
        ],
        compiler_params=PARAMS,
        name="ratio",
    )(inner, near, beyond, point_spread)
    chip_ratio = lax.all_gather(ratio, "core", tiled=True)
    shares = pl.pallas_call(
        back_kernel,
        out_shape=jax.ShapeDtypeStruct((TILES, 8, H * S), F32),
        in_specs=[VM] * 2,
        out_specs=VM,
        scratch_shapes=[
            pltpu.VMEM((H * W + W, E * Z), BF16),
            pltpu.VMEM((H * S, Z), F32),
        ],
        compiler_params=PARAMS,
        name="back",
    )(chip_ratio, point_spread)
    parts = lax.all_to_all(shares, "depth", 0, 0, tiled=True)
    return pl.pallas_call(
        final_kernel,
        out_shape=jax.ShapeDtypeStruct(volume.shape, F32),
        in_specs=[VM, VM],
        out_specs=VM,
        compiler_params=PARAMS,
        name="final",
    )(parts, volume)


def solution(mesh):
    depth, tile = mesh.devices.shape
    split = Mesh(mesh.devices.reshape(depth, tile // 2, 2), ("depth", "pair", "core"))
    spec = P("depth", ("pair", "core"), None)
    return jax.shard_map(body, mesh=split, in_specs=(spec, spec, P()), out_specs=spec, check_vma=False)
```

```python
import jax
import jax.numpy as jnp
from jax import lax
from jax.experimental import pallas as pl
from jax.experimental.pallas import tpu as pltpu
from jax.sharding import Mesh
from jax.sharding import PartitionSpec as P

R = 5
E = 11
Z = 128
TILES = 16
W = 16
H = 8
S = 32
SCALE = 8.0
F32 = jnp.float32
BF16 = jnp.bfloat16
VM = pl.BlockSpec(memory_space=pltpu.VMEM)
PARAMS = pltpu.CompilerParams(vmem_limit_bytes=40 * 1024 * 1024)


def lanes(shape=(8, 128)):
    return lax.broadcasted_iota(jnp.int32, shape, 1)


def pack_kernel(both_ref, out_ref):
    vol_ref, meas_ref = both_ref.at[0], both_ref.at[1]
    lane = lanes()
    slot = lane // S
    inside = lane % S
    rolled = {}

    def turned(ref, key, y, half, shift):
        name = (key, y, half, shift % 128)
        if name not in rolled:
            part = ref[:, y, half * 128 : half * 128 + 128]
            rolled[name] = pltpu.roll(part, shift % 128, 1) if shift % 128 else part
        return rolled[name]

    def window(t, y):
        start = W * t - R
        shift = S * (y % 4) - start
        low, high = max(start, 0) // 128, min(start + W + 2 * R - 1, 255) // 128
        value = turned(vol_ref, 0, y, low, shift)
        if high != low:
            value = jnp.where(inside < 128 - start, value, turned(vol_ref, 0, y, high, shift))
        if start < 0:
            value = jnp.where(inside < -start, 0.0, value)
        if start + W + 2 * R > 256:
            value = jnp.where(inside < 256 - start, value, 0.0)
        return value

    for t in range(TILES):
        for g in range(2):
            value = window(t, 4 * g)
            for s in range(1, 4):
                value = jnp.where(slot < s, value, window(t, 4 * g + s))
            out_ref[t, :, g * 128 : g * 128 + 128] = value.astype(BF16)
    for t in range(TILES):
        value = turned(meas_ref, 1, 0, t // 8, -W * t)
        for y in range(1, H):
            value = jnp.where(lane < W * y, value, turned(meas_ref, 1, y, t // 8, W * y - W * t))
        head = value.astype(BF16)
        out_ref[t, :, 256:384] = head
        out_ref[t, :, 384:512] = (value - head.astype(F32)).astype(BF16)


def group(value, g):
    return value[:, :, g * 128 : g * 128 + 128].astype(F32).reshape(Z, 128)


def join_kernel(own_ref, chip_ref, out_ref):
    core = lax.axis_index("core")
    even = core == 0
    lane = lanes((Z, 128))
    keep = (lane >= 48 * core) & (lane < 80 + 48 * core)
    mate = jnp.where(even, group(chip_ref[1], 0), group(chip_ref[0], 1))
    half = pltpu.roll(mate, 64, 1)
    one = jnp.where(even, pltpu.roll(mate, 96, 1), half)
    two = jnp.where(even, half, pltpu.roll(mate, 32, 1))
    out_ref[:, :, :256] = own_ref[:, :, :256]
    out_ref[:, :, 256:384] = jnp.where(keep, group(own_ref, 2), one).astype(BF16).reshape(TILES, 8, 128)
    out_ref[:, :, 384:] = jnp.where(keep, group(own_ref, 3), two).astype(BF16).reshape(TILES, 8, 128)


def spread_rows(rows_ref, taps_ref, count):
    for y in range(count):
        for b in range(E):
            start = y * S + b
            taps_ref[y * W : y * W + W, b * 128 : b * 128 + 128] = rows_ref[start : start + W, :].astype(BF16)


def add_products(taps_ref, psf_ref, sum_ref, offsets, count, taps_row, sum_rows, first):
    kernel = jnp.concatenate([psf_ref[offset].reshape(E * Z, Z) for offset in offsets], axis=1)
    product = jnp.dot(
        taps_ref[pl.ds(pl.multiple_of(taps_row * W, W), count * W), :], kernel, preferred_element_type=F32
    )
    for i, sum_row in enumerate(sum_rows):
        part = product[:, i * Z : i * Z + Z]
        if i and count == 1:
            break
        if i:
            part = jnp.where(first, part[W:], part[:-W])
        here = pl.ds(pl.multiple_of(sum_row * W, W), (count - i) * W)
        sum_ref[here, :] = sum_ref[here, :] + part


def inner_kernel(own_ref, chip_ref, psf_ref, sum_ref, meas_ref, rows_ref, taps_ref):
    core = lax.axis_index("core")
    for i in range(4):
        rows_ref[i * 128 : i * 128 + 128, :] = group(chip_ref[i // 2], i % 2).T
    meas_ref[...] = (group(own_ref, 2) + group(own_ref, 3)).T
    spread_rows(rows_ref, taps_ref, 2 * H)
    sum_ref[...] = jnp.zeros(sum_ref.shape, F32)
    for k in range(R, -R - 1, -2):
        steps = range(k, max(k - 2, -R - 1), -1)
        add_products(
            taps_ref,
            psf_ref,
            sum_ref,
            [R + i * (1 - 2 * core) for i in steps],
            H + k,
            (H - k) * core,
            [(R - i) * (1 - core) for i in steps],
            core == 1,
        )


def ratio_kernel(inner_ref, meas_ref, next_ref, psf_ref, out_ref, rows_ref, taps_ref, sum_ref):
    core = lax.axis_index("core")
    even = core == 0
    first, second = group(next_ref, 2).T, group(next_ref, 3).T
    shift = 2 * S * (1 - core)
    for g in range(2):
        rows_ref[pl.ds(pl.multiple_of(g * 128 + shift, S), 128), :] = group(next_ref, g).T
    for i, block in enumerate((first, second)):
        at = pl.multiple_of(i * S + 8 * S * core, S)
        rows_ref[pl.ds(at, S), :] = jnp.where(even, block[:S], block[128 - S :])
    spread_rows(rows_ref, taps_ref, 2 * R)
    sum_ref[...] = inner_ref[...]
    for k in range(-R, R, 2):
        steps = (k, k + 1)
        add_products(
            taps_ref,
            psf_ref,
            sum_ref,
            [R + i * (1 - 2 * core) for i in steps],
            R - k,
            (R + k) * (1 - core),
            [(H + i) * core for i in steps],
            even,
        )
    here = pl.ds(pl.multiple_of(R * W * (1 - core), W), H * W)
    out_ref[here, :] = (meas_ref[...] / sum_ref[here, :]).astype(BF16)
    there = pl.ds(pl.multiple_of(H * W * core, W), R * W)
    beyond = first + second
    beyond = jnp.where(even, beyond[(H - R) * W :], beyond[: R * W])
    out_ref[there, :] = (beyond / sum_ref[there, :]).astype(BF16)


def back_kernel(chip_ref, psf_ref, out_ref, rows_ref, sum_ref):
    first_row = lax.axis_index("core") * (H * W)
    for y in range(H + 2 * R):
        value = chip_ref[pl.ds(pl.multiple_of(first_row + y * W, W), W), :]
        for a in range(E):
            row = y + a - 2 * R
            if 0 <= row < H:
                rows_ref[row * W : row * W + W, a * 128 : a * 128 + 128] = value
    rows_ref[H * W : H * W + W, :] = jnp.ones((W, E * Z), BF16)
    sum_ref[...] = jnp.zeros((H * S, Z), F32)
    weight = jnp.zeros((1, Z), F32)
    for first in range(0, E, 2):
        pair = range(first, min(first + 2, E))
        kernel = jnp.concatenate(
            [psf_ref[a, first : first + len(pair)].reshape(len(pair) * Z, Z) for a in range(E)], axis=1
        )
        product = lax.dot_general(rows_ref[...], kernel, (((1,), (1,)), ((), ())), preferred_element_type=F32)
        for i, b in enumerate(pair):
            part = product[:, i * Z : i * Z + Z]
            for y in range(H):
                here = slice(y * S + b, y * S + b + W)
                sum_ref[here, :] = sum_ref[here, :] + part[y * W : y * W + W]
            weight = weight + part[H * W : H * W + 1]
    factor = SCALE / weight
    for g in range(2):
        share = (sum_ref[g * 128 : g * 128 + 128, :] * factor).T
        out_ref[:, :, g * 128 : g * 128 + 128] = share.reshape(TILES, 8, 128)


def final_kernel(parts_ref, vol_ref, out_ref):
    lane = lanes()
    for y in range(H):
        g, s = y // 4, y % 4
        turned = []
        for t in range(TILES):
            part = parts_ref[t, :, g * 128 : g * 128 + 128]
            shift = (W * t - R - S * s) % 128
            turned.append(pltpu.roll(part, shift, 1) if shift else part)
        for half in range(2):
            sums = [None, None]
            for t in range(TILES):
                start, stop = W * t - R - 128 * half, W * t + W + R - 128 * half
                start, stop = max(start, 0), min(stop, 128)
                if start >= stop:
                    continue
                before = sums[t % 2]
                sums[t % 2] = jnp.where(
                    (lane >= start) & (lane < stop), turned[t], 0.0 if before is None else before
                )
            here = slice(half * 128, half * 128 + 128)
            out_ref[:, y, here] = vol_ref[:, y, here] * ((sums[0] + sums[1]) * (1 / SCALE))


def body(volume, measured, point_spread):
    packed = pl.pallas_call(
        pack_kernel,
        out_shape=jax.ShapeDtypeStruct((TILES, 8, 512), BF16),
        in_specs=[VM],
        out_specs=VM,
        compiler_params=PARAMS,
        cost_estimate=pl.CostEstimate(flops=20_000_000_000, bytes_accessed=2**20, transcendentals=0),
        name="pack",
    )(jnp.stack([volume, measured]))
    own = lax.all_to_all(packed, "depth", 0, 0, tiled=True)
    chip = lax.all_gather(own[:, :, :256], "core")
    joined = pl.pallas_call(
        join_kernel,
        out_shape=jax.ShapeDtypeStruct((TILES, 8, 512), BF16),
        in_specs=[VM] * 2,
        out_specs=VM,
        compiler_params=PARAMS,
        name="join",
    )(own, chip)
    tile = ("pair", "core")
    count = lax.axis_size(tile)
    pairs = [(i, i + 1) for i in range(1, count - 1, 2)] + [(i, i - 1) for i in range(2, count, 2)]
    beyond = lax.ppermute(joined, tile, pairs)
    rows = H + R
    inner, near = pl.pallas_call(
        inner_kernel,
        out_shape=[jax.ShapeDtypeStruct((rows * W, Z), F32), jax.ShapeDtypeStruct((H * W, Z), F32)],
        in_specs=[VM] * 3,
        out_specs=[VM] * 2,
        scratch_shapes=[
            pltpu.VMEM((2 * H * S, Z), F32),
            pltpu.VMEM((2 * H * W, E * Z), BF16),
        ],
        compiler_params=PARAMS,
        cost_estimate=pl.CostEstimate(flops=2 * 88 * W * E * Z * Z, bytes_accessed=2**22, transcendentals=0),
        name="inner",
    )(own, chip, point_spread)
    ratio = pl.pallas_call(
        ratio_kernel,
        out_shape=jax.ShapeDtypeStruct((rows * W, Z), BF16),
        in_specs=[VM] * 4,
        out_specs=VM,
        scratch_shapes=[
            pltpu.VMEM((2 * R * S, Z), F32),
            pltpu.VMEM((2 * R * W, E * Z), BF16),
            pltpu.VMEM((rows * W, Z), F32),
        ],
        compiler_params=PARAMS,
        name="ratio",
    )(inner, near, beyond, point_spread)
    chip_ratio = lax.all_gather(ratio, "core", tiled=True)
    shares = pl.pallas_call(
        back_kernel,
        out_shape=jax.ShapeDtypeStruct((TILES, 8, H * S), F32),
        in_specs=[VM] * 2,
        out_specs=VM,
        scratch_shapes=[
            pltpu.VMEM((H * W + W, E * Z), BF16),
            pltpu.VMEM((H * S, Z), F32),
        ],
        compiler_params=PARAMS,
        name="back",
    )(chip_ratio, point_spread)
    parts = lax.all_to_all(shares.astype(jnp.float16), "depth", 0, 0, tiled=True).astype(F32)
    return pl.pallas_call(
        final_kernel,
        out_shape=jax.ShapeDtypeStruct(volume.shape, F32),
        in_specs=[VM, VM],
        out_specs=VM,
        compiler_params=PARAMS,
        name="final",
    )(parts, volume)


def solution(mesh):
    depth, tile = mesh.devices.shape
    split = Mesh(mesh.devices.reshape(depth, tile // 2, 2), ("depth", "pair", "core"))
    spec = P("depth", ("pair", "core"), None)
    return jax.shard_map(body, mesh=split, in_specs=(spec, spec, P()), out_specs=spec, check_vma=False)
```

```python
import jax
import jax.numpy as jnp
from jax import lax
from jax.experimental import pallas as pl
from jax.experimental.pallas import tpu as pltpu
from jax.sharding import Mesh
from jax.sharding import PartitionSpec as P

R = 5
E = 11
Z = 128
TILES = 16
W = 16
H = 8
C = 26
S = 32
SCALE = 8.0
F32 = jnp.float32
BF16 = jnp.bfloat16
F16 = jnp.float16
VM = pl.BlockSpec(memory_space=pltpu.VMEM)
PARAMS = pltpu.CompilerParams(vmem_limit_bytes=40 * 1024 * 1024)


def lanes(shape=(8, 128)):
    return lax.broadcasted_iota(jnp.int32, shape, 1)


def pack_kernel(vol_ref, meas_ref, out_ref):
    even = lax.axis_index("core") == 0
    lane = lanes()
    rows = {}
    rolled = {}

    def row(i, half):
        if (i, half) not in rows:
            here = slice(half * 128, half * 128 + 128)
            a, b = [vol_ref[r // H, :, r % H, here] for r in (i, i + H - R)]
            rows[i, half] = jnp.where(even, a, b).astype(BF16).astype(F32)
        return rows[i, half]

    def turned(part, name, shift):
        name = (*name, shift % 128)
        if name not in rolled:
            rolled[name] = pltpu.roll(part, shift % 128, 1) if shift % 128 else part
        return rolled[name]

    def window(t, i, at):
        start = W * t - R
        low, high = max(start, 0) // 128, min(start + C - 1, 255) // 128
        value = turned(row(i, low), (i, low), at - start)
        if high != low:
            value = jnp.where(lane - at < 128 - start, value, turned(row(i, high), (i, high), at - start))
        if start < 0:
            value = jnp.where(lane - at < -start, 0.0, value)
        if start + C > 256:
            value = jnp.where(lane - at < 256 - start, value, 0.0)
        return value

    def measured(y, half):
        part = meas_ref[:, y, half * 128 : half * 128 + 128]
        return part * part * part * part

    for t in range(TILES):
        for g in range(3):
            value = window(t, 4 * g, 0)
            for s in range(1, 4):
                value = jnp.where(lane < C * s, value, window(t, 4 * g + s, C * s))
            if g < 2:
                value = jnp.where(lane < 4 * C, value, window(t, H + R - 1, 4 * C - 24 * g))
            out_ref[t, :, g * 128 : g * 128 + 128] = value
        half = t // 8
        value = turned(measured(0, half), ("m", 0, half), -W * t)
        for y in range(1, H):
            value = jnp.where(lane < W * y, value, turned(measured(y, half), ("m", y, half), W * y - W * t))
        out_ref[t, :, 384:512] = value


def group(value, g):
    return value[:, :, g * 128 : g * 128 + 128].reshape(Z, 128)


def fill_rows(packed_ref, rows_ref):
    for g in range(3):
        block = group(packed_ref, g).T
        rows_ref[g * 4 * C : (g + 1) * 4 * C, :] = block[: 4 * C]
        if g == 0:
            rows_ref[12 * C : 12 * C + 24, :] = block[4 * C :]
        if g == 1:
            rows_ref[12 * C + 24 : 12 * C + 32, :] = block[4 * C : 4 * C + 8]
    coded = group(packed_ref, 3)
    return jnp.where(coded > 0.0, jnp.sqrt(jnp.sqrt(coded)), 0.0).T


def spread_rows(rows_ref, taps_ref):
    for y in range(H + R):
        for b in range(E):
            start = y * C + b
            taps_ref[y * W : y * W + W, b * 128 : b * 128 + 128] = rows_ref[start : start + W, :].astype(BF16)


def add_products(taps_ref, psf_ref, sum_ref, offsets, count, taps_row, sum_rows, first):
    kernel = jnp.concatenate([psf_ref[offset].reshape(E * Z, Z) for offset in offsets], axis=1)
    product = jnp.dot(
        taps_ref[pl.ds(pl.multiple_of(taps_row * W, W), count * W), :], kernel, preferred_element_type=F32
    )
    for i, sum_row in enumerate(sum_rows):
        part = product[:, i * Z : i * Z + Z]
        if i and count == 1:
            break
        if i:
            part = jnp.where(first, part[W:], part[:-W])
        here = pl.ds(pl.multiple_of(sum_row * W, W), (count - i) * W)
        sum_ref[here, :] = sum_ref[here, :] + part


def inner_kernel(own_ref, psf_ref, sum_ref, meas_ref, rows_ref, taps_ref):
    core = lax.axis_index("core")
    meas_ref[...] = fill_rows(own_ref, rows_ref)
    spread_rows(rows_ref, taps_ref)
    sum_ref[...] = jnp.zeros(sum_ref.shape, F32)
    for k in range(R, -R - 1, -2):
        steps = range(k, max(k - 2, -R - 1), -1)
        add_products(
            taps_ref,
            psf_ref,
            sum_ref,
            [R + i * (1 - 2 * core) for i in steps],
            H + k,
            (R - k) * core,
            [(R - i) * (1 - core) for i in steps],
            core == 1,
        )


def ratio_kernel(inner_ref, meas_ref, next_ref, psf_ref, out_ref, rows_ref, taps_ref, sum_ref):
    core = lax.axis_index("core")
    even = core == 0
    beyond = fill_rows(next_ref, rows_ref)
    spread_rows(rows_ref, taps_ref)
    sum_ref[...] = inner_ref[...]
    for k in range(-R, R, 2):
        steps = (k, k + 1)
        add_products(
            taps_ref,
            psf_ref,
            sum_ref,
            [R + i * (1 - 2 * core) for i in steps],
            R - k,
            (H + k) * (1 - core),
            [(H + i) * core for i in steps],
            even,
        )
    here = pl.ds(pl.multiple_of(R * W * (1 - core), W), H * W)
    out_ref[here, :] = (meas_ref[...] / sum_ref[here, :]).astype(BF16)
    there = pl.ds(pl.multiple_of(H * W * core, W), R * W)
    beyond = jnp.where(even, beyond[(H - R) * W :], beyond[: R * W])
    out_ref[there, :] = (beyond / sum_ref[there, :]).astype(BF16)


def back_kernel(chip_ref, psf_ref, out_ref, rows_ref, sum_ref):
    first_row = lax.axis_index("core") * (H * W)
    for y in range(H + 2 * R):
        value = chip_ref[pl.ds(pl.multiple_of(first_row + y * W, W), W), :]
        for a in range(E):
            row = y + a - 2 * R
            if 0 <= row < H:
                rows_ref[row * W : row * W + W, a * 128 : a * 128 + 128] = value
    rows_ref[H * W : H * W + W, :] = jnp.ones((W, E * Z), BF16)
    sum_ref[...] = jnp.zeros((H * S, Z), F32)
    weight = jnp.zeros((1, Z), F32)
    for first in range(0, E, 2):
        pair = range(first, min(first + 2, E))
        kernel = jnp.concatenate(
            [psf_ref[a, first : first + len(pair)].reshape(len(pair) * Z, Z) for a in range(E)], axis=1
        )
        product = lax.dot_general(rows_ref[...], kernel, (((1,), (1,)), ((), ())), preferred_element_type=F32)
        for i, b in enumerate(pair):
            part = product[:, i * Z : i * Z + Z]
            for y in range(H):
                here = slice(y * S + b, y * S + b + W)
                sum_ref[here, :] = sum_ref[here, :] + part[y * W : y * W + W]
            weight = weight + part[H * W : H * W + 1]
    factor = SCALE / weight
    for g in range(2):
        share = (sum_ref[g * 128 : g * 128 + 128, :] * factor).T
        out_ref[:, :, g * 128 : g * 128 + 128] = share.reshape(TILES, 8, 128)


def final_kernel(parts_ref, vol_ref, out_ref):
    lane = lanes()
    for y in range(H):
        g, s = y // 4, y % 4
        turned = []
        for t in range(TILES):
            part = parts_ref[t, :, g * 128 : g * 128 + 128]
            shift = (W * t - R - S * s) % 128
            turned.append(pltpu.roll(part, shift, 1) if shift else part)
        for half in range(2):
            sums = [None, None]
            for t in range(TILES):
                start, stop = W * t - R - 128 * half, W * t + W + R - 128 * half
                start, stop = max(start, 0), min(stop, 128)
                if start >= stop:
                    continue
                before = sums[t % 2]
                sums[t % 2] = jnp.where(
                    (lane >= start) & (lane < stop), turned[t], 0.0 if before is None else before
                )
            here = slice(half * 128, half * 128 + 128)
            out_ref[:, y, here] = vol_ref[:, y, here] * ((sums[0] + sums[1]) * (1 / SCALE))


def body(volume, measured, point_spread):
    packed = pl.pallas_call(
        pack_kernel,
        out_shape=jax.ShapeDtypeStruct((TILES, 8, 512), F32),
        in_specs=[VM] * 2,
        out_specs=VM,
        compiler_params=PARAMS,
        cost_estimate=pl.CostEstimate(flops=20_000_000_000, bytes_accessed=2**20, transcendentals=0),
        name="pack",
    )(lax.all_gather(volume, "core"), measured)
    own = lax.all_to_all(packed.astype(F16), "depth", 0, 0, tiled=True)
    tile = ("pair", "core")
    count = lax.axis_size(tile)
    pairs = [(i, i + 1) for i in range(1, count - 1, 2)] + [(i, i - 1) for i in range(2, count, 2)]
    beyond = lax.ppermute(own, tile, pairs)
    rows = H + R
    scratch = [pltpu.VMEM((rows * C + 14, Z), F32), pltpu.VMEM((rows * W, E * Z), BF16)]
    inner, near = pl.pallas_call(
        inner_kernel,
        out_shape=[jax.ShapeDtypeStruct((rows * W, Z), F32), jax.ShapeDtypeStruct((H * W, Z), F32)],
        in_specs=[VM] * 2,
        out_specs=[VM] * 2,
        scratch_shapes=scratch,
        compiler_params=PARAMS,
        cost_estimate=pl.CostEstimate(flops=2 * 88 * W * E * Z * Z, bytes_accessed=2**22, transcendentals=0),
        name="inner",
    )(own.astype(F32), point_spread)
    ratio = pl.pallas_call(
        ratio_kernel,
        out_shape=jax.ShapeDtypeStruct((rows * W, Z), BF16),
        in_specs=[VM] * 4,
        out_specs=VM,
        scratch_shapes=[*scratch, pltpu.VMEM((rows * W, Z), F32)],
        compiler_params=PARAMS,
        name="ratio",
    )(inner, near, beyond.astype(F32), point_spread)
    chip_ratio = lax.all_gather(ratio, "core", tiled=True)
    shares = pl.pallas_call(
        back_kernel,
        out_shape=jax.ShapeDtypeStruct((TILES, 8, H * S), F32),
        in_specs=[VM] * 2,
        out_specs=VM,
        scratch_shapes=[
            pltpu.VMEM((H * W + W, E * Z), BF16),
            pltpu.VMEM((H * S, Z), F32),
        ],
        compiler_params=PARAMS,
        name="back",
    )(chip_ratio, point_spread)
    parts = lax.all_to_all(shares.astype(F16), "depth", 0, 0, tiled=True).astype(F32)
    return pl.pallas_call(
        final_kernel,
        out_shape=jax.ShapeDtypeStruct(volume.shape, F32),
        in_specs=[VM, VM],
        out_specs=VM,
        compiler_params=PARAMS,
        name="final",
    )(parts, volume)


def solution(mesh):
    depth, tile = mesh.devices.shape
    split = Mesh(mesh.devices.reshape(depth, tile // 2, 2), ("depth", "pair", "core"))
    spec = P("depth", ("pair", "core"), None)
    return jax.shard_map(body, mesh=split, in_specs=(spec, spec, P()), out_specs=spec, check_vma=False)
```

```python
import jax
import jax.numpy as jnp
from jax import lax
from jax.experimental import pallas as pl
from jax.experimental.pallas import tpu as pltpu
from jax.sharding import Mesh
from jax.sharding import PartitionSpec as P

R = 5
E = 11
Z = 128
TILES = 16
W = 16
H = 8
C = 26
S = 32
SCALE = 8.0
F32 = jnp.float32
BF16 = jnp.bfloat16
F16 = jnp.float16
VM = pl.BlockSpec(memory_space=pltpu.VMEM)
PARAMS = pltpu.CompilerParams(vmem_limit_bytes=40 * 1024 * 1024)


def lanes(shape=(8, 128)):
    return lax.broadcasted_iota(jnp.int32, shape, 1)


VOLUME_AT = [(0, C * i) for i in range(4)] + [(1, C * i) for i in range(4)]
VOLUME_AT += [(2, 64 + C * i) for i in range(2)] + [(3, 48 + C * i) for i in range(3)]
MEASURED_AT = [(2, W * i) for i in range(4)] + [(0, 4 * C)] + [(3, W * i) for i in range(3)]


def pack_kernel(vol_ref, meas_ref, out_ref):
    even = lax.axis_index("core") == 0
    lane = lanes()
    rows = {}
    rolled = {}

    def volume_row(j, half):
        here = slice(half * 128, half * 128 + 128)
        odd = j + 6 if j < 2 * R else j - 7
        a, b = [vol_ref[r // H, :, r % H, here] for r in (j, odd)]
        return jnp.where(even, a, b).astype(BF16).astype(F32)

    def measured_row(j, half):
        here = slice(half * 128, half * 128 + 128)
        odd = j + 3 if j < R else j - R
        part = jnp.where(even, meas_ref[:, j, here], meas_ref[:, odd, here])
        part = part * part
        return part * part

    def turned(make, j, half, shift):
        name = (make, j, half)
        if name not in rows:
            rows[name] = make(j, half)
        shift = shift % 128
        if (name, shift) not in rolled:
            rolled[name, shift] = pltpu.roll(rows[name], shift, 1) if shift else rows[name]
        return rolled[name, shift]

    def window(t, j, at):
        start = W * t - R
        low, high = max(start, 0) // 128, min(start + C - 1, 255) // 128
        value = turned(volume_row, j, low, at - start)
        if high != low:
            value = jnp.where(lane - at < 128 - start, value, turned(volume_row, j, high, at - start))
        if start < 0:
            value = jnp.where(lane - at < -start, 0.0, value)
        if start + C > 256:
            value = jnp.where(lane - at < 256 - start, value, 0.0)
        return value

    for t in range(TILES):
        for g in range(4):
            parts = [(at, window(t, j, at)) for j, (where, at) in enumerate(VOLUME_AT) if where == g]
            parts += [
                (at, turned(measured_row, j, t // 8, at - W * t)) for j, (where, at) in enumerate(MEASURED_AT) if where == g
            ]
            parts.sort(key=lambda part: part[0])
            value = parts[0][1]
            for at, part in parts[1:]:
                value = jnp.where(lane < at, value, part)
            out_ref[t, :, g * 128 : g * 128 + 128] = value


def turned_groups(packed_ref, count):
    return [packed_ref[:, :, g * 128 : g * 128 + 128].reshape(Z, 128).T for g in range(count)]


def decoded(value):
    return jnp.where(value > 0.0, jnp.sqrt(jnp.sqrt(value)), 0.0)


def fill_first_rows(blocks, rows_ref):
    rows_ref[: 4 * C, :] = blocks[0][: 4 * C]
    rows_ref[4 * C : 8 * C, :] = blocks[1][: 4 * C]
    rows_ref[8 * C : 8 * C + 56, :] = blocks[2][64:120]


def spread_row(rows_ref, taps_ref, start, row):
    here = pl.ds(pl.multiple_of(row * W, W), W)
    for b in range(E):
        taps_ref[here, b * 128 : b * 128 + 128] = rows_ref[start + b : start + b + W, :].astype(BF16)


def add_products(taps_ref, psf_ref, sum_ref, offsets, count, taps_row, sum_rows, first):
    kernel = jnp.concatenate([psf_ref[offset].reshape(E * Z, Z) for offset in offsets], axis=1)
    product = jnp.dot(
        taps_ref[pl.ds(pl.multiple_of(taps_row * W, W), count * W), :], kernel, preferred_element_type=F32
    )
    for i, sum_row in enumerate(sum_rows):
        part = product[:, i * Z : i * Z + Z]
        if i and count == 1:
            break
        if i:
            part = jnp.where(first, part[W:], part[:-W])
        here = pl.ds(pl.multiple_of(sum_row * W, W), (count - i) * W)
        sum_ref[here, :] = sum_ref[here, :] + part


def inner_kernel(own_ref, psf_ref, sum_ref, meas_ref, rows_ref, taps_ref):
    core = lax.axis_index("core")
    blocks = turned_groups(own_ref, 4)
    fill_first_rows(blocks, rows_ref)
    rows_ref[264:344, :] = blocks[3][48:]
    for j in range(H + R):
        if j < 2 * R:
            spread_row(rows_ref, taps_ref, j * C, j + 3 * core)
        else:
            spread_row(rows_ref, taps_ref, 264 + (j - 2 * R) * C, j - 2 * R * core)
    for part, even_row, odd_row in ((blocks[2][:64], 0, 3), (blocks[0][4 * C : 4 * C + W], 4, 7), (blocks[3][:48], 5, 0)):
        row = even_row + (odd_row - even_row) * core
        meas_ref[pl.ds(pl.multiple_of(row * W, W), part.shape[0]), :] = decoded(part)
    sum_ref[...] = jnp.zeros(sum_ref.shape, F32)
    for k in range(R, -R - 1, -2):
        steps = range(k, max(k - 2, -R - 1), -1)
        add_products(
            taps_ref,
            psf_ref,
            sum_ref,
            [R + i * (1 - 2 * core) for i in steps],
            H + k,
            (R - k) * core,
            [(R - i) * (1 - core) for i in steps],
            core == 1,
        )


def ratio_kernel(inner_ref, meas_ref, next_ref, psf_ref, out_ref, rows_ref, taps_ref, sum_ref):
    core = lax.axis_index("core")
    even = core == 0
    blocks = turned_groups(next_ref, 3)
    fill_first_rows(blocks, rows_ref)
    for j in range(2 * R):
        spread_row(rows_ref, taps_ref, j * C, j)
    sum_ref[...] = inner_ref[...]
    for k in range(-R, R, 2):
        steps = (k, k + 1)
        add_products(
            taps_ref,
            psf_ref,
            sum_ref,
            [R + i * (1 - 2 * core) for i in steps],
            R - k,
            (R + k) * (1 - core),
            [(H + i) * core for i in steps],
            even,
        )
    here = pl.ds(pl.multiple_of(R * W * (1 - core), W), H * W)
    out_ref[here, :] = (meas_ref[...] / sum_ref[here, :]).astype(BF16)
    there = H * W * core
    for part, row in ((blocks[2][:64], 0), (blocks[0][4 * C : 4 * C + W], 4)):
        here = pl.ds(pl.multiple_of(there + row * W, W), part.shape[0])
        out_ref[here, :] = (decoded(part) / sum_ref[here, :]).astype(BF16)


def back_kernel(chip_ref, psf_ref, out_ref, rows_ref, sum_ref):
    first_row = lax.axis_index("core") * (H * W)
    for y in range(H + 2 * R):
        value = chip_ref[pl.ds(pl.multiple_of(first_row + y * W, W), W), :]
        for a in range(E):
            row = y + a - 2 * R
            if 0 <= row < H:
                rows_ref[row * W : row * W + W, a * 128 : a * 128 + 128] = value
    rows_ref[H * W : H * W + W, :] = jnp.ones((W, E * Z), BF16)
    sum_ref[...] = jnp.zeros((H * S, Z), F32)
    weight = jnp.zeros((1, Z), F32)
    for first in range(0, E, 2):
        pair = range(first, min(first + 2, E))
        kernel = jnp.concatenate(
            [psf_ref[a, first : first + len(pair)].reshape(len(pair) * Z, Z) for a in range(E)], axis=1
        )
        product = lax.dot_general(rows_ref[...], kernel, (((1,), (1,)), ((), ())), preferred_element_type=F32)
        for i, b in enumerate(pair):
            part = product[:, i * Z : i * Z + Z]
            for y in range(H):
                here = slice(y * S + b, y * S + b + W)
                sum_ref[here, :] = sum_ref[here, :] + part[y * W : y * W + W]
            weight = weight + part[H * W : H * W + 1]
    factor = SCALE / weight
    for g in range(2):
        share = (sum_ref[g * 128 : g * 128 + 128, :] * factor).T
        out_ref[:, :, g * 128 : g * 128 + 128] = share.reshape(TILES, 8, 128)


def final_kernel(parts_ref, vol_ref, out_ref):
    lane = lanes()
    for y in range(H):
        g, s = y // 4, y % 4
        turned = []
        for t in range(TILES):
            part = parts_ref[t, :, g * 128 : g * 128 + 128]
            shift = (W * t - R - S * s) % 128
            turned.append(pltpu.roll(part, shift, 1) if shift else part)
        for half in range(2):
            sums = [None, None]
            for t in range(TILES):
                start, stop = W * t - R - 128 * half, W * t + W + R - 128 * half
                start, stop = max(start, 0), min(stop, 128)
                if start >= stop:
                    continue
                before = sums[t % 2]
                sums[t % 2] = jnp.where(
                    (lane >= start) & (lane < stop), turned[t], 0.0 if before is None else before
                )
            here = slice(half * 128, half * 128 + 128)
            out_ref[:, y, here] = vol_ref[:, y, here] * ((sums[0] + sums[1]) * (1 / SCALE))


def body(volume, measured, point_spread):
    packed = pl.pallas_call(
        pack_kernel,
        out_shape=jax.ShapeDtypeStruct((TILES, 8, 512), F32),
        in_specs=[VM] * 2,
        out_specs=VM,
        compiler_params=PARAMS,
        cost_estimate=pl.CostEstimate(flops=20_000_000_000, bytes_accessed=2**20, transcendentals=0),
        name="pack",
    )(lax.all_gather(volume, "core"), measured)
    own = lax.all_to_all(packed.astype(F16), "depth", 0, 0, tiled=True)
    tile = ("pair", "core")
    count = lax.axis_size(tile)
    pairs = [(i, i + 1) for i in range(1, count - 1, 2)] + [(i, i - 1) for i in range(2, count, 2)]
    beyond = lax.ppermute(own[:, :, :384], tile, pairs)
    rows = H + R
    scratch = [pltpu.VMEM((rows * C + 14, Z), F32), pltpu.VMEM((rows * W, E * Z), BF16)]
    inner, near = pl.pallas_call(
        inner_kernel,
        out_shape=[jax.ShapeDtypeStruct((rows * W, Z), F32), jax.ShapeDtypeStruct((H * W, Z), F32)],
        in_specs=[VM] * 2,
        out_specs=[VM] * 2,
        scratch_shapes=scratch,
        compiler_params=PARAMS,
        cost_estimate=pl.CostEstimate(flops=2 * 88 * W * E * Z * Z, bytes_accessed=2**22, transcendentals=0),
        name="inner",
    )(own.astype(F32), point_spread)
    ratio = pl.pallas_call(
        ratio_kernel,
        out_shape=jax.ShapeDtypeStruct((rows * W, Z), BF16),
        in_specs=[VM] * 4,
        out_specs=VM,
        scratch_shapes=[*scratch, pltpu.VMEM((rows * W, Z), F32)],
        compiler_params=PARAMS,
        name="ratio",
    )(inner, near, beyond.astype(F32), point_spread)
    chip_ratio = lax.all_gather(ratio, "core", tiled=True)
    shares = pl.pallas_call(
        back_kernel,
        out_shape=jax.ShapeDtypeStruct((TILES, 8, H * S), F32),
        in_specs=[VM] * 2,
        out_specs=VM,
        scratch_shapes=[
            pltpu.VMEM((H * W + W, E * Z), BF16),
            pltpu.VMEM((H * S, Z), F32),
        ],
        compiler_params=PARAMS,
        name="back",
    )(chip_ratio, point_spread)
    parts = lax.all_to_all(shares.astype(F16), "depth", 0, 0, tiled=True).astype(F32)
    return pl.pallas_call(
        final_kernel,
        out_shape=jax.ShapeDtypeStruct(volume.shape, F32),
        in_specs=[VM, VM],
        out_specs=VM,
        compiler_params=PARAMS,
        name="final",
    )(parts, volume)


def solution(mesh):
    depth, tile = mesh.devices.shape
    split = Mesh(mesh.devices.reshape(depth, tile // 2, 2), ("depth", "pair", "core"))
    spec = P("depth", ("pair", "core"), None)
    return jax.shard_map(body, mesh=split, in_specs=(spec, spec, P()), out_specs=spec, check_vma=False)
```

```python
import jax
import jax.numpy as jnp
from jax import lax
from jax.experimental import pallas as pl
from jax.experimental.pallas import tpu as pltpu
from jax.sharding import Mesh
from jax.sharding import PartitionSpec as P

R = 5
E = 11
Z = 128
TILES = 16
W = 16
H = 8
C = 26
S = 32
SCALE = 8.0
F32 = jnp.float32
BF16 = jnp.bfloat16
F16 = jnp.float16
VM = pl.BlockSpec(memory_space=pltpu.VMEM)
PARAMS = pltpu.CompilerParams(vmem_limit_bytes=40 * 1024 * 1024)


def lanes(shape=(8, 128)):
    return lax.broadcasted_iota(jnp.int32, shape, 1)


VOLUME_AT = [(0, C * i) for i in range(4)] + [(1, C * i) for i in range(4)]
VOLUME_AT += [(2, 64 + C * i) for i in range(2)] + [(3, 48 + C * i) for i in range(3)]
MEASURED_AT = [(2, W * i) for i in range(4)] + [(0, 4 * C)] + [(3, W * i) for i in range(3)]


def pack_kernel(both_ref, mate_ref, out_ref):
    vol_ref, meas_ref = both_ref.at[0], both_ref.at[1]
    even = lax.axis_index("core") == 0
    lane = lanes()
    rows = {}
    rolled = {}

    def volume_row(j, half):
        here = slice(half * 128, half * 128 + 128)
        a = vol_ref[:, j, here] if j < H else mate_ref[:, j - H, here]
        if j < 2 * R:
            b = mate_ref[:, j + 6, here] if j < 2 else vol_ref[:, j - 2, here]
        else:
            b = mate_ref[:, j - 7, here]
        return jnp.where(even, a, b).astype(BF16).astype(F32)

    def measured_row(j, half):
        here = slice(half * 128, half * 128 + 128)
        odd = j + 3 if j < R else j - R
        part = jnp.where(even, meas_ref[:, j, here], meas_ref[:, odd, here])
        part = part * part
        return part * part

    def turned(make, j, half, shift):
        name = (make, j, half)
        if name not in rows:
            rows[name] = make(j, half)
        shift = shift % 128
        if (name, shift) not in rolled:
            rolled[name, shift] = pltpu.roll(rows[name], shift, 1) if shift else rows[name]
        return rolled[name, shift]

    def window(t, j, at):
        start = W * t - R
        low, high = max(start, 0) // 128, min(start + C - 1, 255) // 128
        value = turned(volume_row, j, low, at - start)
        if high != low:
            value = jnp.where(lane - at < 128 - start, value, turned(volume_row, j, high, at - start))
        if start < 0:
            value = jnp.where(lane - at < -start, 0.0, value)
        if start + C > 256:
            value = jnp.where(lane - at < 256 - start, value, 0.0)
        return value

    for t in range(TILES):
        for g in range(4):
            parts = [(at, window(t, j, at)) for j, (where, at) in enumerate(VOLUME_AT) if where == g]
            parts += [
                (at, turned(measured_row, j, t // 8, at - W * t)) for j, (where, at) in enumerate(MEASURED_AT) if where == g
            ]
            parts.sort(key=lambda part: part[0])
            value = parts[0][1]
            for at, part in parts[1:]:
                value = jnp.where(lane < at, value, part)
            out_ref[t, :, g * 128 : g * 128 + 128] = value


def turned_groups(packed_ref, count):
    return [packed_ref[:, :, g * 128 : g * 128 + 128].reshape(Z, 128).T for g in range(count)]


def decoded(value):
    return jnp.where(value > 0.0, jnp.sqrt(jnp.sqrt(value)), 0.0)


def fill_first_rows(blocks, rows_ref):
    rows_ref[: 4 * C, :] = blocks[0][: 4 * C]
    rows_ref[4 * C : 8 * C, :] = blocks[1][: 4 * C]
    rows_ref[8 * C : 8 * C + 56, :] = blocks[2][64:120]


def spread_row(rows_ref, taps_ref, start, row):
    here = pl.ds(pl.multiple_of(row * W, W), W)
    for b in range(E):
        taps_ref[here, b * 128 : b * 128 + 128] = rows_ref[start + b : start + b + W, :].astype(BF16)


def add_products(taps_ref, psf_ref, sum_ref, offsets, count, taps_row, sum_rows, first):
    kernel = jnp.concatenate([psf_ref[offset].reshape(E * Z, Z) for offset in offsets], axis=1)
    product = jnp.dot(
        taps_ref[pl.ds(pl.multiple_of(taps_row * W, W), count * W), :], kernel, preferred_element_type=F32
    )
    for i, sum_row in enumerate(sum_rows):
        part = product[:, i * Z : i * Z + Z]
        if i and count == 1:
            break
        if i:
            part = jnp.where(first, part[W:], part[:-W])
        here = pl.ds(pl.multiple_of(sum_row * W, W), (count - i) * W)
        sum_ref[here, :] = sum_ref[here, :] + part


def inner_kernel(own_ref, psf_ref, sum_ref, meas_ref, rows_ref, taps_ref):
    core = lax.axis_index("core")
    blocks = turned_groups(own_ref, 4)
    fill_first_rows(blocks, rows_ref)
    rows_ref[264:344, :] = blocks[3][48:]
    for j in range(H + R):
        if j < 2 * R:
            spread_row(rows_ref, taps_ref, j * C, j + 3 * core)
        else:
            spread_row(rows_ref, taps_ref, 264 + (j - 2 * R) * C, j - 2 * R * core)
    for part, even_row, odd_row in ((blocks[2][:64], 0, 3), (blocks[0][4 * C : 4 * C + W], 4, 7), (blocks[3][:48], 5, 0)):
        row = even_row + (odd_row - even_row) * core
        meas_ref[pl.ds(pl.multiple_of(row * W, W), part.shape[0]), :] = decoded(part)
    sum_ref[...] = jnp.zeros(sum_ref.shape, F32)
    for k in range(R, -R - 1, -2):
        steps = range(k, max(k - 2, -R - 1), -1)
        add_products(
            taps_ref,
            psf_ref,
            sum_ref,
            [R + i * (1 - 2 * core) for i in steps],
            H + k,
            (R - k) * core,
            [(R - i) * (1 - core) for i in steps],
            core == 1,
        )


def ratio_kernel(inner_ref, meas_ref, next_ref, psf_ref, out_ref, rows_ref, taps_ref, sum_ref):
    core = lax.axis_index("core")
    even = core == 0
    blocks = turned_groups(next_ref, 3)
    fill_first_rows(blocks, rows_ref)
    for j in range(2 * R):
        spread_row(rows_ref, taps_ref, j * C, j)
    sum_ref[...] = inner_ref[...]
    for k in range(-R, R, 2):
        steps = (k, k + 1)
        add_products(
            taps_ref,
            psf_ref,
            sum_ref,
            [R + i * (1 - 2 * core) for i in steps],
            R - k,
            (R + k) * (1 - core),
            [(H + i) * core for i in steps],
            even,
        )
    here = pl.ds(pl.multiple_of(R * W * (1 - core), W), H * W)
    out_ref[here, :] = (meas_ref[...] / sum_ref[here, :]).astype(BF16)
    there = H * W * core
    for part, row in ((blocks[2][:64], 0), (blocks[0][4 * C : 4 * C + W], 4)):
        here = pl.ds(pl.multiple_of(there + row * W, W), part.shape[0])
        out_ref[here, :] = (decoded(part) / sum_ref[here, :]).astype(BF16)


def back_kernel(chip_ref, psf_ref, out_ref, rows_ref, sum_ref):
    first_row = lax.axis_index("core") * (H * W)
    for y in range(H + 2 * R):
        value = chip_ref[pl.ds(pl.multiple_of(first_row + y * W, W), W), :]
        for a in range(E):
            row = y + a - 2 * R
            if 0 <= row < H:
                rows_ref[row * W : row * W + W, a * 128 : a * 128 + 128] = value
    rows_ref[H * W : H * W + W, :] = jnp.ones((W, E * Z), BF16)
    sum_ref[...] = jnp.zeros((H * S, Z), F32)
    weight = jnp.zeros((1, Z), F32)
    for first in range(0, E, 2):
        pair = range(first, min(first + 2, E))
        kernel = jnp.concatenate(
            [psf_ref[a, first : first + len(pair)].reshape(len(pair) * Z, Z) for a in range(E)], axis=1
        )
        product = lax.dot_general(rows_ref[...], kernel, (((1,), (1,)), ((), ())), preferred_element_type=F32)
        for i, b in enumerate(pair):
            part = product[:, i * Z : i * Z + Z]
            for y in range(H):
                here = slice(y * S + b, y * S + b + W)
                sum_ref[here, :] = sum_ref[here, :] + part[y * W : y * W + W]
            weight = weight + part[H * W : H * W + 1]
    factor = SCALE / weight
    for g in range(2):
        share = (sum_ref[g * 128 : g * 128 + 128, :] * factor).T
        out_ref[:, :, g * 128 : g * 128 + 128] = share.reshape(TILES, 8, 128)


def final_kernel(parts_ref, vol_ref, out_ref):
    lane = lanes()
    for y in range(H):
        g, s = y // 4, y % 4
        turned = []
        for t in range(TILES):
            part = parts_ref[t, :, g * 128 : g * 128 + 128]
            shift = (W * t - R - S * s) % 128
            turned.append(pltpu.roll(part, shift, 1) if shift else part)
        for half in range(2):
            sums = [None, None]
            for t in range(TILES):
                start, stop = W * t - R - 128 * half, W * t + W + R - 128 * half
                start, stop = max(start, 0), min(stop, 128)
                if start >= stop:
                    continue
                before = sums[t % 2]
                sums[t % 2] = jnp.where(
                    (lane >= start) & (lane < stop), turned[t], 0.0 if before is None else before
                )
            here = slice(half * 128, half * 128 + 128)
            out_ref[:, y, here] = vol_ref[:, y, here] * ((sums[0] + sums[1]) * (1 / SCALE))


def body(volume, measured, point_spread):
    packed = pl.pallas_call(
        pack_kernel,
        out_shape=jax.ShapeDtypeStruct((TILES, 8, 512), F32),
        in_specs=[VM] * 2,
        out_specs=VM,
        compiler_params=PARAMS,
        cost_estimate=pl.CostEstimate(flops=20_000_000_000, bytes_accessed=2**20, transcendentals=0),
        name="pack",
    )(jnp.stack([volume, measured]), lax.ppermute(volume, "core", [(0, 1), (1, 0)]))
    own = lax.all_to_all(packed.astype(F16), "depth", 0, 0, tiled=True)
    tile = ("pair", "core")
    count = lax.axis_size(tile)
    pairs = [(i, i + 1) for i in range(1, count - 1, 2)] + [(i, i - 1) for i in range(2, count, 2)]
    beyond = lax.ppermute(own[:, :, :384], tile, pairs)
    rows = H + R
    scratch = [pltpu.VMEM((rows * C + 14, Z), F32), pltpu.VMEM((rows * W, E * Z), BF16)]
    inner, near = pl.pallas_call(
        inner_kernel,
        out_shape=[jax.ShapeDtypeStruct((rows * W, Z), F32), jax.ShapeDtypeStruct((H * W, Z), F32)],
        in_specs=[VM] * 2,
        out_specs=[VM] * 2,
        scratch_shapes=scratch,
        compiler_params=PARAMS,
        cost_estimate=pl.CostEstimate(flops=2 * 88 * W * E * Z * Z, bytes_accessed=2**22, transcendentals=0),
        name="inner",
    )(own.astype(F32), point_spread)
    ratio = pl.pallas_call(
        ratio_kernel,
        out_shape=jax.ShapeDtypeStruct((rows * W, Z), BF16),
        in_specs=[VM] * 4,
        out_specs=VM,
        scratch_shapes=[*scratch, pltpu.VMEM((rows * W, Z), F32)],
        compiler_params=PARAMS,
        name="ratio",
    )(inner, near, beyond.astype(F32), point_spread)
    chip_ratio = lax.all_gather(ratio, "core", tiled=True)
    shares = pl.pallas_call(
        back_kernel,
        out_shape=jax.ShapeDtypeStruct((TILES, 8, H * S), F32),
        in_specs=[VM] * 2,
        out_specs=VM,
        scratch_shapes=[
            pltpu.VMEM((H * W + W, E * Z), BF16),
            pltpu.VMEM((H * S, Z), F32),
        ],
        compiler_params=PARAMS,
        name="back",
    )(chip_ratio, point_spread)
    parts = lax.all_to_all(shares.astype(F16), "depth", 0, 0, tiled=True).astype(F32)
    return pl.pallas_call(
        final_kernel,
        out_shape=jax.ShapeDtypeStruct(volume.shape, F32),
        in_specs=[VM, VM],
        out_specs=VM,
        compiler_params=PARAMS,
        name="final",
    )(parts, volume)


def solution(mesh):
    depth, tile = mesh.devices.shape
    split = Mesh(mesh.devices.reshape(depth, tile // 2, 2), ("depth", "pair", "core"))
    spec = P("depth", ("pair", "core"), None)
    return jax.shard_map(body, mesh=split, in_specs=(spec, spec, P()), out_specs=spec, check_vma=False)
```

```python
import jax
import jax.numpy as jnp
from jax import lax
from jax.experimental import pallas as pl
from jax.experimental.pallas import tpu as pltpu
from jax.sharding import Mesh
from jax.sharding import PartitionSpec as P

R = 5
E = 11
Z = 128
TILES = 16
W = 16
H = 8
C = 26
S = 32
SCALE = 8.0
F32 = jnp.float32
BF16 = jnp.bfloat16
F16 = jnp.float16
VM = pl.BlockSpec(memory_space=pltpu.VMEM)
PARAMS = pltpu.CompilerParams(vmem_limit_bytes=40 * 1024 * 1024)


def lanes(shape=(8, 128)):
    return lax.broadcasted_iota(jnp.int32, shape, 1)


VOLUME_AT = [(0, C * i) for i in range(4)] + [(1, C * i) for i in range(4)]
VOLUME_AT += [(2, 64 + C * i) for i in range(2)] + [(3, 48 + C * i) for i in range(3)]
MEASURED_AT = [(2, W * i) for i in range(4)] + [(0, 4 * C)] + [(3, W * i) for i in range(3)]


def mark_kernel(out_ref):
    out_ref[...] = jnp.zeros(out_ref.shape, F32)


def pack_kernel(vol_ref, meas_ref, out_ref):
    even = lax.axis_index("core") == 0
    lane = lanes()
    rows = {}
    rolled = {}

    def volume_row(j, half):
        here = slice(half * 128, half * 128 + 128)
        odd = j + 6 if j < 2 * R else j - 7
        a, b = [vol_ref[r // H, :, r % H, here] for r in (j, odd)]
        return jnp.where(even, a, b).astype(BF16).astype(F32)

    def measured_row(j, half):
        here = slice(half * 128, half * 128 + 128)
        odd = j + 3 if j < R else j - R
        part = jnp.where(even, meas_ref[:, j, here], meas_ref[:, odd, here])
        part = part * part
        return part * part

    def turned(make, j, half, shift):
        name = (make, j, half)
        if name not in rows:
            rows[name] = make(j, half)
        shift = shift % 128
        if (name, shift) not in rolled:
            rolled[name, shift] = pltpu.roll(rows[name], shift, 1) if shift else rows[name]
        return rolled[name, shift]

    def window(t, j, at):
        start = W * t - R
        low, high = max(start, 0) // 128, min(start + C - 1, 255) // 128
        value = turned(volume_row, j, low, at - start)
        if high != low:
            value = jnp.where(lane - at < 128 - start, value, turned(volume_row, j, high, at - start))
        if start < 0:
            value = jnp.where(lane - at < -start, 0.0, value)
        if start + C > 256:
            value = jnp.where(lane - at < 256 - start, value, 0.0)
        return value

    for t in range(TILES):
        for g in range(4):
            parts = [(at, window(t, j, at)) for j, (where, at) in enumerate(VOLUME_AT) if where == g]
            parts += [
                (at, turned(measured_row, j, t // 8, at - W * t)) for j, (where, at) in enumerate(MEASURED_AT) if where == g
            ]
            parts.sort(key=lambda part: part[0])
            value = parts[0][1]
            for at, part in parts[1:]:
                value = jnp.where(lane < at, value, part)
            out_ref[t, :, g * 128 : g * 128 + 128] = value


def turned_groups(packed_ref, count):
    return [packed_ref[:, :, g * 128 : g * 128 + 128].reshape(Z, 128).T for g in range(count)]


def decoded(value):
    return jnp.where(value > 0.0, jnp.sqrt(jnp.sqrt(value)), 0.0)


def fill_first_rows(blocks, rows_ref):
    rows_ref[: 4 * C, :] = blocks[0][: 4 * C]
    rows_ref[4 * C : 8 * C, :] = blocks[1][: 4 * C]
    rows_ref[8 * C : 8 * C + 56, :] = blocks[2][64:120]


def spread_row(rows_ref, taps_ref, start, row):
    here = pl.ds(pl.multiple_of(row * W, W), W)
    for b in range(E):
        taps_ref[here, b * 128 : b * 128 + 128] = rows_ref[start + b : start + b + W, :].astype(BF16)


def add_products(taps_ref, psf_ref, sum_ref, offsets, count, taps_row, sum_rows, first):
    kernel = jnp.concatenate([psf_ref[offset].reshape(E * Z, Z) for offset in offsets], axis=1)
    product = jnp.dot(
        taps_ref[pl.ds(pl.multiple_of(taps_row * W, W), count * W), :], kernel, preferred_element_type=F32
    )
    for i, sum_row in enumerate(sum_rows):
        part = product[:, i * Z : i * Z + Z]
        if i and count == 1:
            break
        if i:
            part = jnp.where(first, part[W:], part[:-W])
        here = pl.ds(pl.multiple_of(sum_row * W, W), (count - i) * W)
        sum_ref[here, :] = sum_ref[here, :] + part


def inner_kernel(own_ref, psf_ref, sum_ref, meas_ref, rows_ref, taps_ref):
    core = lax.axis_index("core")
    blocks = turned_groups(own_ref, 4)
    fill_first_rows(blocks, rows_ref)
    rows_ref[264:344, :] = blocks[3][48:]
    for j in range(H + R):
        if j < 2 * R:
            spread_row(rows_ref, taps_ref, j * C, j + 3 * core)
        else:
            spread_row(rows_ref, taps_ref, 264 + (j - 2 * R) * C, j - 2 * R * core)
    for part, even_row, odd_row in ((blocks[2][:64], 0, 3), (blocks[0][4 * C : 4 * C + W], 4, 7), (blocks[3][:48], 5, 0)):
        row = even_row + (odd_row - even_row) * core
        meas_ref[pl.ds(pl.multiple_of(row * W, W), part.shape[0]), :] = decoded(part)
    sum_ref[...] = jnp.zeros(sum_ref.shape, F32)
    for k in range(R, -R - 1, -2):
        steps = range(k, max(k - 2, -R - 1), -1)
        add_products(
            taps_ref,
            psf_ref,
            sum_ref,
            [R + i * (1 - 2 * core) for i in steps],
            H + k,
            (R - k) * core,
            [(R - i) * (1 - core) for i in steps],
            core == 1,
        )


def ratio_kernel(inner_ref, meas_ref, next_ref, psf_ref, out_ref, rows_ref, taps_ref, sum_ref):
    core = lax.axis_index("core")
    even = core == 0
    blocks = turned_groups(next_ref, 3)
    fill_first_rows(blocks, rows_ref)
    for j in range(2 * R):
        spread_row(rows_ref, taps_ref, j * C, j)
    sum_ref[...] = inner_ref[...]
    for k in range(-R, R, 2):
        steps = (k, k + 1)
        add_products(
            taps_ref,
            psf_ref,
            sum_ref,
            [R + i * (1 - 2 * core) for i in steps],
            R - k,
            (R + k) * (1 - core),
            [(H + i) * core for i in steps],
            even,
        )
    here = pl.ds(pl.multiple_of(R * W * (1 - core), W), H * W)
    out_ref[here, :] = (meas_ref[...] / sum_ref[here, :]).astype(BF16)
    there = H * W * core
    for part, row in ((blocks[2][:64], 0), (blocks[0][4 * C : 4 * C + W], 4)):
        here = pl.ds(pl.multiple_of(there + row * W, W), part.shape[0])
        out_ref[here, :] = (decoded(part) / sum_ref[here, :]).astype(BF16)


def back_kernel(chip_ref, psf_ref, out_ref, rows_ref, sum_ref):
    first_row = lax.axis_index("core") * (H * W)
    for y in range(H + 2 * R):
        value = chip_ref[pl.ds(pl.multiple_of(first_row + y * W, W), W), :]
        for a in range(E):
            row = y + a - 2 * R
            if 0 <= row < H:
                rows_ref[row * W : row * W + W, a * 128 : a * 128 + 128] = value
    rows_ref[H * W : H * W + W, :] = jnp.ones((W, E * Z), BF16)
    sum_ref[...] = jnp.zeros((H * S, Z), F32)
    weight = jnp.zeros((1, Z), F32)
    for first in range(0, E, 2):
        pair = range(first, min(first + 2, E))
        kernel = jnp.concatenate(
            [psf_ref[a, first : first + len(pair)].reshape(len(pair) * Z, Z) for a in range(E)], axis=1
        )
        product = lax.dot_general(rows_ref[...], kernel, (((1,), (1,)), ((), ())), preferred_element_type=F32)
        for i, b in enumerate(pair):
            part = product[:, i * Z : i * Z + Z]
            for y in range(H):
                here = slice(y * S + b, y * S + b + W)
                sum_ref[here, :] = sum_ref[here, :] + part[y * W : y * W + W]
            weight = weight + part[H * W : H * W + 1]
    factor = SCALE / weight
    for g in range(2):
        share = (sum_ref[g * 128 : g * 128 + 128, :] * factor).T
        out_ref[:, :, g * 128 : g * 128 + 128] = share.reshape(TILES, 8, 128)


def final_kernel(parts_ref, vol_ref, mark_ref, out_ref):
    lane = lanes()
    for y in range(H):
        g, s = y // 4, y % 4
        turned = []
        for t in range(TILES):
            part = parts_ref[t, :, g * 128 : g * 128 + 128]
            shift = (W * t - R - S * s) % 128
            turned.append(pltpu.roll(part, shift, 1) if shift else part)
        for half in range(2):
            sums = [None, None]
            for t in range(TILES):
                start, stop = W * t - R - 128 * half, W * t + W + R - 128 * half
                start, stop = max(start, 0), min(stop, 128)
                if start >= stop:
                    continue
                before = sums[t % 2]
                sums[t % 2] = jnp.where(
                    (lane >= start) & (lane < stop), turned[t], 0.0 if before is None else before
                )
            here = slice(half * 128, half * 128 + 128)
            out_ref[:, y, here] = vol_ref[:, y, here] * ((sums[0] + sums[1]) * (1 / SCALE))


def body(volume, measured, point_spread):
    mark = pl.pallas_call(
        mark_kernel,
        out_shape=jax.ShapeDtypeStruct((8, 128), F32),
        out_specs=VM,
        cost_estimate=pl.CostEstimate(flops=20_000_000_000, bytes_accessed=2**20, transcendentals=0),
        name="mark",
    )()
    volume_first, mark = lax.optimization_barrier((volume, mark))
    packed = pl.pallas_call(
        pack_kernel,
        out_shape=jax.ShapeDtypeStruct((TILES, 8, 512), F32),
        in_specs=[VM] * 2,
        out_specs=VM,
        compiler_params=PARAMS,
        cost_estimate=pl.CostEstimate(flops=20_000_000_000, bytes_accessed=2**20, transcendentals=0),
        name="pack",
    )(lax.all_gather(volume_first, "core"), measured)
    own = lax.all_to_all(packed.astype(F16), "depth", 0, 0, tiled=True)
    tile = ("pair", "core")
    count = lax.axis_size(tile)
    pairs = [(i, i + 1) for i in range(1, count - 1, 2)] + [(i, i - 1) for i in range(2, count, 2)]
    beyond = lax.ppermute(own[:, :, :384], tile, pairs)
    rows = H + R
    scratch = [pltpu.VMEM((rows * C + 14, Z), F32), pltpu.VMEM((rows * W, E * Z), BF16)]
    inner, near = pl.pallas_call(
        inner_kernel,
        out_shape=[jax.ShapeDtypeStruct((rows * W, Z), F32), jax.ShapeDtypeStruct((H * W, Z), F32)],
        in_specs=[VM] * 2,
        out_specs=[VM] * 2,
        scratch_shapes=scratch,
        compiler_params=PARAMS,
        cost_estimate=pl.CostEstimate(flops=2 * 88 * W * E * Z * Z, bytes_accessed=2**22, transcendentals=0),
        name="inner",
    )(own.astype(F32), point_spread)
    ratio = pl.pallas_call(
        ratio_kernel,
        out_shape=jax.ShapeDtypeStruct((rows * W, Z), BF16),
        in_specs=[VM] * 4,
        out_specs=VM,
        scratch_shapes=[*scratch, pltpu.VMEM((rows * W, Z), F32)],
        compiler_params=PARAMS,
        name="ratio",
    )(inner, near, beyond.astype(F32), point_spread)
    chip_ratio = lax.all_gather(ratio, "core", tiled=True)
    shares = pl.pallas_call(
        back_kernel,
        out_shape=jax.ShapeDtypeStruct((TILES, 8, H * S), F32),
        in_specs=[VM] * 2,
        out_specs=VM,
        scratch_shapes=[
            pltpu.VMEM((H * W + W, E * Z), BF16),
            pltpu.VMEM((H * S, Z), F32),
        ],
        compiler_params=PARAMS,
        name="back",
    )(chip_ratio, point_spread)
    parts = lax.all_to_all(shares.astype(F16), "depth", 0, 0, tiled=True).astype(F32)
    return pl.pallas_call(
        final_kernel,
        out_shape=jax.ShapeDtypeStruct(volume.shape, F32),
        in_specs=[VM, VM, pl.BlockSpec(memory_space=pl.ANY)],
        out_specs=VM,
        compiler_params=PARAMS,
        name="final",
    )(parts, volume, mark)


def solution(mesh):
    depth, tile = mesh.devices.shape
    split = Mesh(mesh.devices.reshape(depth, tile // 2, 2), ("depth", "pair", "core"))
    spec = P("depth", ("pair", "core"), None)
    return jax.shard_map(body, mesh=split, in_specs=(spec, spec, P()), out_specs=spec, check_vma=False)
```

```python
import jax
import jax.numpy as jnp
from jax import lax
from jax.experimental import pallas as pl
from jax.experimental.pallas import tpu as pltpu
from jax.sharding import Mesh
from jax.sharding import PartitionSpec as P

R = 5
E = 11
Z = 128
TILES = 16
W = 16
H = 8
C = 26
S = 32
SCALE = 8.0
F32 = jnp.float32
BF16 = jnp.bfloat16
F16 = jnp.float16
VM = pl.BlockSpec(memory_space=pltpu.VMEM)
PARAMS = pltpu.CompilerParams(vmem_limit_bytes=40 * 1024 * 1024)


def lanes(shape=(8, 128)):
    return lax.broadcasted_iota(jnp.int32, shape, 1)


def pack_kernel(both_ref, out_ref):
    vol_ref, meas_ref = both_ref.at[0], both_ref.at[1]
    lane = lanes()
    rows = {}
    rolled = {}

    def volume_row(y, half):
        return vol_ref[:, y, half * 128 : half * 128 + 128].astype(BF16).astype(F32)

    def measured_row(y, half):
        part = meas_ref[:, y, half * 128 : half * 128 + 128]
        part = part * part
        return part * part

    def turned(make, y, half, shift):
        name = (make, y, half)
        if name not in rows:
            rows[name] = make(y, half)
        shift = shift % 128
        if (name, shift) not in rolled:
            rolled[name, shift] = pltpu.roll(rows[name], shift, 1) if shift else rows[name]
        return rolled[name, shift]

    def window(t, y, at):
        start = W * t - R
        low, high = max(start, 0) // 128, min(start + C - 1, 255) // 128
        value = turned(volume_row, y, low, at - start)
        if high != low:
            value = jnp.where(lane - at < 128 - start, value, turned(volume_row, y, high, at - start))
        if start < 0:
            value = jnp.where(lane - at < -start, 0.0, value)
        if start + C > 256:
            value = jnp.where(lane - at < 256 - start, value, 0.0)
        return value

    for t in range(TILES):
        for g in range(2):
            value = window(t, 4 * g, 0)
            for i in range(1, 4):
                value = jnp.where(lane < C * i, value, window(t, 4 * g + i, C * i))
            out_ref[t, :, g * 128 : g * 128 + 128] = value
        value = turned(measured_row, 0, t // 8, -W * t)
        for y in range(1, H):
            value = jnp.where(lane < W * y, value, turned(measured_row, y, t // 8, W * y - W * t))
        out_ref[t, :, 256:] = value


def join_kernel(chip_ref, out_ref):
    core = lax.axis_index("core")
    even = core == 0
    lane = lanes((Z, 128))

    def group(i, g):
        return chip_ref[i, :, :, g * 128 : g * 128 + 128].reshape(Z, 128)

    def place(when_even, when_odd):
        return jnp.where(even, pltpu.roll(mate, when_even, 1), pltpu.roll(mate, when_odd, 1))

    own = [jnp.where(even, group(0, g), group(1, g)) for g in range(3)]
    mate = jnp.where(even, group(1, 0), group(0, 1))
    keep = (lane >= 48 * core) & (lane < 80 + 48 * core)
    parts = [
        jnp.where(lane < 4 * C, own[0], place(78, 26)),
        jnp.where(lane < 4 * C, own[1], place(54, 2)),
        jnp.where(keep, own[2], place(80, 76)),
    ]
    for g, part in enumerate(parts):
        out_ref[:, :, g * 128 : g * 128 + 128] = part.reshape(TILES, 8, 128)


def turned_groups(packed, count):
    return [packed[:, :, g * 128 : g * 128 + 128].reshape(Z, 128).T for g in range(count)]


def decoded(value):
    return jnp.where(value > 0.0, jnp.sqrt(jnp.sqrt(value)), 0.0)


def spread_row(rows_ref, taps_ref, start, row):
    here = pl.ds(pl.multiple_of(row * W, W), W)
    for b in range(E):
        taps_ref[here, b * 128 : b * 128 + 128] = rows_ref[start + b : start + b + W, :].astype(BF16)


def add_products(taps_ref, psf_ref, sum_ref, offsets, count, taps_row, sum_rows, first):
    kernel = jnp.concatenate([psf_ref[offset].reshape(E * Z, Z) for offset in offsets], axis=1)
    product = jnp.dot(
        taps_ref[pl.ds(pl.multiple_of(taps_row * W, W), count * W), :], kernel, preferred_element_type=F32
    )
    for i, sum_row in enumerate(sum_rows):
        part = product[:, i * Z : i * Z + Z]
        if i and count == 1:
            break
        if i:
            part = jnp.where(first, part[W:], part[:-W])
        here = pl.ds(pl.multiple_of(sum_row * W, W), (count - i) * W)
        sum_ref[here, :] = sum_ref[here, :] + part


def inner_kernel(chip_ref, psf_ref, sum_ref, meas_ref, rows_ref, taps_ref):
    core = lax.axis_index("core")
    for i in range(2):
        for g, block in enumerate(turned_groups(chip_ref.at[i], 2)):
            start = (2 * i + g) * 4 * C
            rows_ref[start : start + 4 * C, :] = block[: 4 * C]
    for y in range(2 * H):
        spread_row(rows_ref, taps_ref, y * C, y)
    coded = jnp.where(core == 0, chip_ref[0, :, :, 256:], chip_ref[1, :, :, 256:])
    meas_ref[...] = decoded(coded.reshape(Z, 128)).T
    sum_ref[...] = jnp.zeros(sum_ref.shape, F32)
    for k in range(R, -R - 1, -2):
        steps = range(k, max(k - 2, -R - 1), -1)
        add_products(
            taps_ref,
            psf_ref,
            sum_ref,
            [R + i * (1 - 2 * core) for i in steps],
            H + k,
            (H - k) * core,
            [(R - i) * (1 - core) for i in steps],
            core == 1,
        )


def ratio_kernel(inner_ref, meas_ref, next_ref, psf_ref, out_ref, rows_ref, taps_ref, sum_ref):
    core = lax.axis_index("core")
    even = core == 0
    blocks = turned_groups(next_ref, 3)
    rows_ref[: 4 * C, :] = blocks[0][: 4 * C]
    rows_ref[4 * C : 8 * C, :] = blocks[1][: 4 * C]
    rows_ref[208:240, :] = jnp.where(even, blocks[2][:32], blocks[2][80:112])
    rows_ref[240:264, :] = blocks[0][4 * C :]
    rows_ref[264:272, :] = blocks[1][4 * C : 4 * C + 8]
    for y in range(H):
        spread_row(rows_ref, taps_ref, y * C, y + 2 - 2 * core)
    spread_row(rows_ref, taps_ref, 208, H * core)
    spread_row(rows_ref, taps_ref, 240, H * core + 1)
    sum_ref[...] = inner_ref[...]
    for k in range(-R, R, 2):
        steps = (k, k + 1)
        add_products(
            taps_ref,
            psf_ref,
            sum_ref,
            [R + i * (1 - 2 * core) for i in steps],
            R - k,
            (R + k) * (1 - core),
            [(H + i) * core for i in steps],
            even,
        )
    here = pl.ds(pl.multiple_of(R * W * (1 - core), W), H * W)
    out_ref[here, :] = (meas_ref[...] / sum_ref[here, :]).astype(BF16)
    there = pl.ds(pl.multiple_of(H * W * core, W), R * W)
    beyond = decoded(jnp.where(even, blocks[2][(H - R) * W :], blocks[2][: R * W]))
    out_ref[there, :] = (beyond / sum_ref[there, :]).astype(BF16)


def back_kernel(chip_ref, psf_ref, out_ref, rows_ref, sum_ref):
    first_row = lax.axis_index("core") * (H * W)
    for y in range(H + 2 * R):
        value = chip_ref[pl.ds(pl.multiple_of(first_row + y * W, W), W), :]
        for a in range(E):
            row = y + a - 2 * R
            if 0 <= row < H:
                rows_ref[row * W : row * W + W, a * 128 : a * 128 + 128] = value
    rows_ref[H * W : H * W + W, :] = jnp.ones((W, E * Z), BF16)
    sum_ref[...] = jnp.zeros((H * S, Z), F32)
    weight = jnp.zeros((1, Z), F32)
    for first in range(0, E, 2):
        pair = range(first, min(first + 2, E))
        kernel = jnp.concatenate(
            [psf_ref[a, first : first + len(pair)].reshape(len(pair) * Z, Z) for a in range(E)], axis=1
        )
        product = lax.dot_general(rows_ref[...], kernel, (((1,), (1,)), ((), ())), preferred_element_type=F32)
        for i, b in enumerate(pair):
            part = product[:, i * Z : i * Z + Z]
            for y in range(H):
                here = slice(y * S + b, y * S + b + W)
                sum_ref[here, :] = sum_ref[here, :] + part[y * W : y * W + W]
            weight = weight + part[H * W : H * W + 1]
    factor = SCALE / weight
    for g in range(2):
        share = (sum_ref[g * 128 : g * 128 + 128, :] * factor).T
        out_ref[:, :, g * 128 : g * 128 + 128] = share.reshape(TILES, 8, 128)


def final_kernel(parts_ref, vol_ref, out_ref):
    lane = lanes()
    for y in range(H):
        g, s = y // 4, y % 4
        turned = []
        for t in range(TILES):
            part = parts_ref[t, :, g * 128 : g * 128 + 128]
            shift = (W * t - R - S * s) % 128
            turned.append(pltpu.roll(part, shift, 1) if shift else part)
        for half in range(2):
            sums = [None, None]
            for t in range(TILES):
                start, stop = W * t - R - 128 * half, W * t + W + R - 128 * half
                start, stop = max(start, 0), min(stop, 128)
                if start >= stop:
                    continue
                before = sums[t % 2]
                sums[t % 2] = jnp.where(
                    (lane >= start) & (lane < stop), turned[t], 0.0 if before is None else before
                )
            here = slice(half * 128, half * 128 + 128)
            out_ref[:, y, here] = vol_ref[:, y, here] * ((sums[0] + sums[1]) * (1 / SCALE))


def body(volume, measured, point_spread):
    packed = pl.pallas_call(
        pack_kernel,
        out_shape=jax.ShapeDtypeStruct((TILES, 8, 384), F32),
        in_specs=[VM],
        out_specs=VM,
        compiler_params=PARAMS,
        cost_estimate=pl.CostEstimate(flops=20_000_000_000, bytes_accessed=2**20, transcendentals=0),
        name="pack",
    )(jnp.stack([volume, measured]))
    own = lax.all_to_all(packed.astype(F16), "depth", 0, 0, tiled=True)
    chip = lax.all_gather(own, "core").astype(F32)
    joined = pl.pallas_call(
        join_kernel,
        out_shape=jax.ShapeDtypeStruct((TILES, 8, 384), F32),
        in_specs=[VM],
        out_specs=VM,
        compiler_params=PARAMS,
        name="join",
    )(chip)
    tile = ("pair", "core")
    count = lax.axis_size(tile)
    pairs = [(i, i + 1) for i in range(1, count - 1, 2)] + [(i, i - 1) for i in range(2, count, 2)]
    beyond = lax.ppermute(joined.astype(F16), tile, pairs)
    rows = H + R
    scratch = [pltpu.VMEM((2 * H * C, Z), F32), pltpu.VMEM((2 * H * W, E * Z), BF16)]
    inner, near = pl.pallas_call(
        inner_kernel,
        out_shape=[jax.ShapeDtypeStruct((rows * W, Z), F32), jax.ShapeDtypeStruct((H * W, Z), F32)],
        in_specs=[VM] * 2,
        out_specs=[VM] * 2,
        scratch_shapes=scratch,
        compiler_params=PARAMS,
        cost_estimate=pl.CostEstimate(flops=2 * 88 * W * E * Z * Z, bytes_accessed=2**22, transcendentals=0),
        name="inner",
    )(chip, point_spread)
    ratio = pl.pallas_call(
        ratio_kernel,
        out_shape=jax.ShapeDtypeStruct((rows * W, Z), BF16),
        in_specs=[VM] * 4,
        out_specs=VM,
        scratch_shapes=[*scratch, pltpu.VMEM((rows * W, Z), F32)],
        compiler_params=PARAMS,
        name="ratio",
    )(inner, near, beyond.astype(F32), point_spread)
    chip_ratio = lax.all_gather(ratio, "core", tiled=True)
    shares = pl.pallas_call(
        back_kernel,
        out_shape=jax.ShapeDtypeStruct((TILES, 8, H * S), F32),
        in_specs=[VM] * 2,
        out_specs=VM,
        scratch_shapes=[
            pltpu.VMEM((H * W + W, E * Z), BF16),
            pltpu.VMEM((H * S, Z), F32),
        ],
        compiler_params=PARAMS,
        name="back",
    )(chip_ratio, point_spread)
    parts = lax.all_to_all(shares.astype(F16), "depth", 0, 0, tiled=True).astype(F32)
    return pl.pallas_call(
        final_kernel,
        out_shape=jax.ShapeDtypeStruct(volume.shape, F32),
        in_specs=[VM, VM],
        out_specs=VM,
        compiler_params=PARAMS,
        name="final",
    )(parts, volume)


def solution(mesh):
    depth, tile = mesh.devices.shape
    split = Mesh(mesh.devices.reshape(depth, tile // 2, 2), ("depth", "pair", "core"))
    spec = P("depth", ("pair", "core"), None)
    return jax.shard_map(body, mesh=split, in_specs=(spec, spec, P()), out_specs=spec, check_vma=False)
```

```python
import jax
import jax.numpy as jnp
from jax import lax
from jax.experimental import pallas as pl
from jax.experimental.pallas import tpu as pltpu
from jax.sharding import Mesh
from jax.sharding import PartitionSpec as P

R = 5
E = 11
Z = 128
TILES = 16
W = 16
H = 8
C = 26
S = 32
SCALE = 8.0
F32 = jnp.float32
BF16 = jnp.bfloat16
F16 = jnp.float16
VM = pl.BlockSpec(memory_space=pltpu.VMEM)
PARAMS = pltpu.CompilerParams(vmem_limit_bytes=40 * 1024 * 1024)


def lanes(shape=(8, 128)):
    return lax.broadcasted_iota(jnp.int32, shape, 1)


VOLUME_AT = [(0, C * i) for i in range(4)] + [(1, C * i) for i in range(4)]
VOLUME_AT += [(2, 64 + C * i) for i in range(2)] + [(3, 48 + C * i) for i in range(3)]
MEASURED_AT = [(2, W * i) for i in range(4)] + [(0, 4 * C)] + [(3, W * i) for i in range(3)]


def mark_kernel(out_ref):
    out_ref[...] = jnp.zeros(out_ref.shape, F32)


def pack_kernel(vol_ref, meas_ref, out_ref):
    even = lax.axis_index("core") == 0
    lane = lanes()
    rows = {}
    rolled = {}

    def volume_row(j, half):
        here = slice(half * 128, half * 128 + 128)
        odd = j + 6 if j < 2 * R else j - 7
        a, b = [vol_ref[r // H, :, r % H, here] for r in (j, odd)]
        return jnp.where(even, a, b).astype(BF16).astype(F32)

    def measured_row(j, half):
        here = slice(half * 128, half * 128 + 128)
        odd = j + 3 if j < R else j - R
        part = jnp.where(even, meas_ref[:, j, here], meas_ref[:, odd, here])
        part = part * part
        return part * part

    def turned(make, j, half, shift):
        name = (make, j, half)
        if name not in rows:
            rows[name] = make(j, half)
        shift = shift % 128
        if (name, shift) not in rolled:
            rolled[name, shift] = pltpu.roll(rows[name], shift, 1) if shift else rows[name]
        return rolled[name, shift]

    def window(t, j, at):
        start = W * t - R
        low, high = max(start, 0) // 128, min(start + C - 1, 255) // 128
        value = turned(volume_row, j, low, at - start)
        if high != low:
            value = jnp.where(lane - at < 128 - start, value, turned(volume_row, j, high, at - start))
        if start < 0:
            value = jnp.where(lane - at < -start, 0.0, value)
        if start + C > 256:
            value = jnp.where(lane - at < 256 - start, value, 0.0)
        return value

    for t in range(TILES):
        for g in range(4):
            parts = [(at, window(t, j, at)) for j, (where, at) in enumerate(VOLUME_AT) if where == g]
            parts += [
                (at, turned(measured_row, j, t // 8, at - W * t)) for j, (where, at) in enumerate(MEASURED_AT) if where == g
            ]
            parts.sort(key=lambda part: part[0])
            value = parts[0][1]
            for at, part in parts[1:]:
                value = jnp.where(lane < at, value, part)
            out_ref[t, :, g * 128 : g * 128 + 128] = value


def turned_groups(packed_ref, count):
    return [packed_ref[:, :, g * 128 : g * 128 + 128].reshape(Z, 128).T for g in range(count)]


def decoded(value):
    return jnp.where(value > 0.0, jnp.sqrt(jnp.sqrt(value)), 0.0)


def fill_first_rows(blocks, rows_ref):
    rows_ref[: 4 * C, :] = blocks[0][: 4 * C]
    rows_ref[4 * C : 8 * C, :] = blocks[1][: 4 * C]
    rows_ref[8 * C : 8 * C + 56, :] = blocks[2][64:120]


def spread_row(rows_ref, taps_ref, start, row):
    here = pl.ds(pl.multiple_of(row * W, W), W)
    for b in range(E):
        taps_ref[here, b * 128 : b * 128 + 128] = rows_ref[start + b : start + b + W, :].astype(BF16)


def add_products(taps_ref, psf_ref, sum_ref, offsets, count, taps_row, sum_rows, first):
    kernel = jnp.concatenate([psf_ref[offset].reshape(E * Z, Z) for offset in offsets], axis=1)
    product = jnp.dot(
        taps_ref[pl.ds(pl.multiple_of(taps_row * W, W), count * W), :], kernel, preferred_element_type=F32
    )
    for i, sum_row in enumerate(sum_rows):
        part = product[:, i * Z : i * Z + Z]
        if i and count == 1:
            break
        if i:
            part = jnp.where(first, part[W:], part[:-W])
        here = pl.ds(pl.multiple_of(sum_row * W, W), (count - i) * W)
        sum_ref[here, :] = sum_ref[here, :] + part


def inner_kernel(own_ref, psf_ref, sum_ref, meas_ref, rows_ref, taps_ref):
    core = lax.axis_index("core")
    blocks = turned_groups(own_ref, 4)
    fill_first_rows(blocks, rows_ref)
    rows_ref[264:344, :] = blocks[3][48:]
    for j in range(H + R):
        if j < 2 * R:
            spread_row(rows_ref, taps_ref, j * C, j + 3 * core)
        else:
            spread_row(rows_ref, taps_ref, 264 + (j - 2 * R) * C, j - 2 * R * core)
    for part, even_row, odd_row in ((blocks[2][:64], 0, 3), (blocks[0][4 * C : 4 * C + W], 4, 7), (blocks[3][:48], 5, 0)):
        row = even_row + (odd_row - even_row) * core
        meas_ref[pl.ds(pl.multiple_of(row * W, W), part.shape[0]), :] = decoded(part)
    sum_ref[...] = jnp.zeros(sum_ref.shape, F32)
    for k in range(R, -R - 1, -2):
        steps = range(k, max(k - 2, -R - 1), -1)
        add_products(
            taps_ref,
            psf_ref,
            sum_ref,
            [R + i * (1 - 2 * core) for i in steps],
            H + k,
            (R - k) * core,
            [(R - i) * (1 - core) for i in steps],
            core == 1,
        )


def ratio_kernel(inner_ref, meas_ref, next_ref, psf_ref, out_ref, rows_ref, taps_ref, sum_ref):
    core = lax.axis_index("core")
    even = core == 0
    blocks = turned_groups(next_ref, 3)
    fill_first_rows(blocks, rows_ref)
    for j in range(2 * R):
        spread_row(rows_ref, taps_ref, j * C, j)
    sum_ref[...] = inner_ref[...]
    for k in range(-R, R, 2):
        steps = (k, k + 1)
        add_products(
            taps_ref,
            psf_ref,
            sum_ref,
            [R + i * (1 - 2 * core) for i in steps],
            R - k,
            (R + k) * (1 - core),
            [(H + i) * core for i in steps],
            even,
        )
    here = pl.ds(pl.multiple_of(R * W * (1 - core), W), H * W)
    out_ref[here, :] = (meas_ref[...] / sum_ref[here, :]).astype(BF16)
    there = H * W * core
    for part, row in ((blocks[2][:64], 0), (blocks[0][4 * C : 4 * C + W], 4)):
        here = pl.ds(pl.multiple_of(there + row * W, W), part.shape[0])
        out_ref[here, :] = (decoded(part) / sum_ref[here, :]).astype(BF16)


def back_kernel(chip_ref, psf_ref, out_ref, rows_ref, sum_ref):
    first_row = lax.axis_index("core") * (H * W)
    for y in range(H + 2 * R):
        value = chip_ref[pl.ds(pl.multiple_of(first_row + y * W, W), W), :]
        for a in range(E):
            row = y + a - 2 * R
            if 0 <= row < H:
                rows_ref[row * W : row * W + W, a * 128 : a * 128 + 128] = value
    rows_ref[H * W : H * W + W, :] = jnp.ones((W, E * Z), BF16)
    sum_ref[...] = jnp.zeros((H * S, Z), F32)
    weight = jnp.zeros((1, Z), F32)
    for first in range(0, E, 2):
        pair = range(first, min(first + 2, E))
        kernel = jnp.concatenate(
            [psf_ref[a, first : first + len(pair)].reshape(len(pair) * Z, Z) for a in range(E)], axis=1
        )
        product = lax.dot_general(rows_ref[...], kernel, (((1,), (1,)), ((), ())), preferred_element_type=F32)
        for i, b in enumerate(pair):
            part = product[:, i * Z : i * Z + Z]
            for y in range(H):
                here = slice(y * S + b, y * S + b + W)
                sum_ref[here, :] = sum_ref[here, :] + part[y * W : y * W + W]
            weight = weight + part[H * W : H * W + 1]
    factor = SCALE / weight
    for g in range(2):
        share = (sum_ref[g * 128 : g * 128 + 128, :] * factor).T
        out_ref[:, :, g * 128 : g * 128 + 128] = share.reshape(TILES, 8, 128)


def final_kernel(parts_ref, vol_ref, mark_ref, out_hbm, out_ref, sems):
    lane = lanes()
    copies = []
    for half in range(2):
        here = slice(half * 128, half * 128 + 128)
        for y in range(H):
            g, s = y // 4, y % 4
            sums = [None, None]
            for t in range(TILES):
                start, stop = W * t - R - 128 * half, W * t + W + R - 128 * half
                start, stop = max(start, 0), min(stop, 128)
                if start >= stop:
                    continue
                part = parts_ref[t, :, g * 128 : g * 128 + 128]
                shift = (W * t - R - S * s) % 128
                part = pltpu.roll(part, shift, 1) if shift else part
                before = sums[t % 2]
                sums[t % 2] = jnp.where((lane >= start) & (lane < stop), part, 0.0 if before is None else before)
            out_ref[:, y, here] = vol_ref[:, y, here] * ((sums[0] + sums[1]) * (1 / SCALE))
        copies.append(pltpu.make_async_copy(out_ref.at[:, :, here], out_hbm.at[:, :, here], sems.at[half]))
        copies[-1].start()
    for copy in copies:
        copy.wait()


def body(volume, measured, point_spread):
    mark = pl.pallas_call(
        mark_kernel,
        out_shape=jax.ShapeDtypeStruct((8, 128), F32),
        out_specs=VM,
        cost_estimate=pl.CostEstimate(flops=20_000_000_000, bytes_accessed=2**20, transcendentals=0),
        name="mark",
    )()
    volume_first, mark = lax.optimization_barrier((volume, mark))
    packed = pl.pallas_call(
        pack_kernel,
        out_shape=jax.ShapeDtypeStruct((TILES, 8, 512), F32),
        in_specs=[VM] * 2,
        out_specs=VM,
        compiler_params=PARAMS,
        cost_estimate=pl.CostEstimate(flops=20_000_000_000, bytes_accessed=2**20, transcendentals=0),
        name="pack",
    )(lax.all_gather(volume_first, "core"), measured)
    own = lax.all_to_all(packed.astype(F16), "depth", 0, 0, tiled=True)
    tile = ("pair", "core")
    count = lax.axis_size(tile)
    pairs = [(i, i + 1) for i in range(1, count - 1, 2)] + [(i, i - 1) for i in range(2, count, 2)]
    beyond = lax.ppermute(own[:, :, :384], tile, pairs)
    rows = H + R
    scratch = [pltpu.VMEM((rows * C + 14, Z), F32), pltpu.VMEM((rows * W, E * Z), BF16)]
    inner, near = pl.pallas_call(
        inner_kernel,
        out_shape=[jax.ShapeDtypeStruct((rows * W, Z), F32), jax.ShapeDtypeStruct((H * W, Z), F32)],
        in_specs=[VM] * 2,
        out_specs=[VM] * 2,
        scratch_shapes=scratch,
        compiler_params=PARAMS,
        cost_estimate=pl.CostEstimate(flops=2 * 88 * W * E * Z * Z, bytes_accessed=2**22, transcendentals=0),
        name="inner",
    )(own.astype(F32), point_spread)
    ratio = pl.pallas_call(
        ratio_kernel,
        out_shape=jax.ShapeDtypeStruct((rows * W, Z), BF16),
        in_specs=[VM] * 4,
        out_specs=VM,
        scratch_shapes=[*scratch, pltpu.VMEM((rows * W, Z), F32)],
        compiler_params=PARAMS,
        name="ratio",
    )(inner, near, beyond.astype(F32), point_spread)
    chip_ratio = lax.all_gather(ratio, "core", tiled=True)
    shares = pl.pallas_call(
        back_kernel,
        out_shape=jax.ShapeDtypeStruct((TILES, 8, H * S), F32),
        in_specs=[VM] * 2,
        out_specs=VM,
        scratch_shapes=[
            pltpu.VMEM((H * W + W, E * Z), BF16),
            pltpu.VMEM((H * S, Z), F32),
        ],
        compiler_params=PARAMS,
        name="back",
    )(chip_ratio, point_spread)
    parts = lax.all_to_all(shares.astype(F16), "depth", 0, 0, tiled=True).astype(F32)
    return pl.pallas_call(
        final_kernel,
        out_shape=jax.ShapeDtypeStruct(volume.shape, F32),
        in_specs=[VM, VM, pl.BlockSpec(memory_space=pl.ANY)],
        out_specs=pl.BlockSpec(memory_space=pl.ANY),
        scratch_shapes=[pltpu.VMEM(volume.shape, F32), pltpu.SemaphoreType.DMA((2,))],
        compiler_params=PARAMS,
        name="final",
    )(parts, volume, mark)


def solution(mesh):
    depth, tile = mesh.devices.shape
    split = Mesh(mesh.devices.reshape(depth, tile // 2, 2), ("depth", "pair", "core"))
    spec = P("depth", ("pair", "core"), None)
    return jax.shard_map(body, mesh=split, in_specs=(spec, spec, P()), out_specs=spec, check_vma=False)
```

```python
import jax
import jax.numpy as jnp
from jax import lax
from jax.experimental import pallas as pl
from jax.experimental.pallas import tpu as pltpu
from jax.sharding import Mesh
from jax.sharding import PartitionSpec as P

R = 5
E = 11
Z = 128
TILES = 16
W = 16
H = 8
C = 26
S = 32
SCALE = 8.0
F32 = jnp.float32
BF16 = jnp.bfloat16
F16 = jnp.float16
VM = pl.BlockSpec(memory_space=pltpu.VMEM)
PARAMS = pltpu.CompilerParams(vmem_limit_bytes=40 * 1024 * 1024)


def lanes(shape=(8, 128)):
    return lax.broadcasted_iota(jnp.int32, shape, 1)


VOLUME_AT = [(0, C * i) for i in range(4)] + [(1, C * i) for i in range(4)]
VOLUME_AT += [(2, 64 + C * i) for i in range(2)] + [(3, 48 + C * i) for i in range(3)]
MEASURED_AT = [(2, W * i) for i in range(4)] + [(0, 4 * C)] + [(3, W * i) for i in range(3)]


def mark_kernel(out_ref):
    out_ref[...] = jnp.zeros(out_ref.shape, F32)


def pack_kernel(vol_ref, meas_ref, out_ref):
    even = lax.axis_index("core") == 0
    lane = lanes()
    rows = {}
    rolled = {}

    def volume_row(j, half):
        here = slice(half * 128, half * 128 + 128)
        odd = j + 6 if j < 2 * R else j - 7
        a, b = [vol_ref[r // H, :, r % H, here] for r in (j, odd)]
        return jnp.where(even, a, b).astype(BF16).astype(F32)

    def measured_row(j, half):
        here = slice(half * 128, half * 128 + 128)
        odd = j + 3 if j < R else j - R
        part = jnp.where(even, meas_ref[:, j, here], meas_ref[:, odd, here])
        part = part * part
        return part * part

    def turned(make, j, half, shift):
        name = (make, j, half)
        if name not in rows:
            rows[name] = make(j, half)
        shift = shift % 128
        if (name, shift) not in rolled:
            rolled[name, shift] = pltpu.roll(rows[name], shift, 1) if shift else rows[name]
        return rolled[name, shift]

    def window(t, j, at):
        start = W * t - R
        low, high = max(start, 0) // 128, min(start + C - 1, 255) // 128
        value = turned(volume_row, j, low, at - start)
        if high != low:
            value = jnp.where(lane - at < 128 - start, value, turned(volume_row, j, high, at - start))
        if start < 0:
            value = jnp.where(lane - at < -start, 0.0, value)
        if start + C > 256:
            value = jnp.where(lane - at < 256 - start, value, 0.0)
        return value

    for t in range(TILES):
        for g in range(4):
            parts = [(at, window(t, j, at)) for j, (where, at) in enumerate(VOLUME_AT) if where == g]
            parts += [
                (at, turned(measured_row, j, t // 8, at - W * t)) for j, (where, at) in enumerate(MEASURED_AT) if where == g
            ]
            parts.sort(key=lambda part: part[0])
            value = parts[0][1]
            for at, part in parts[1:]:
                value = jnp.where(lane < at, value, part)
            out_ref[t, :, g * 128 : g * 128 + 128] = value


def turned_groups(packed_ref, count):
    return [packed_ref[:, :, g * 128 : g * 128 + 128].reshape(Z, 128).T for g in range(count)]


def decoded(value):
    return jnp.where(value > 0.0, jnp.sqrt(jnp.sqrt(value)), 0.0)


def fill_first_rows(blocks, rows_ref):
    rows_ref[: 4 * C, :] = blocks[0][: 4 * C]
    rows_ref[4 * C : 8 * C, :] = blocks[1][: 4 * C]
    rows_ref[8 * C : 8 * C + 56, :] = blocks[2][64:120]


def spread_row(rows_ref, taps_ref, start, row):
    here = pl.ds(pl.multiple_of(row * W, W), W)
    for b in range(E):
        taps_ref[here, b * 128 : b * 128 + 128] = rows_ref[start + b : start + b + W, :].astype(BF16)


def add_products(taps_ref, psf_ref, sum_ref, offsets, count, taps_row, sum_rows, first):
    kernel = jnp.concatenate([psf_ref[offset].reshape(E * Z, Z) for offset in offsets], axis=1)
    product = jnp.dot(
        taps_ref[pl.ds(pl.multiple_of(taps_row * W, W), count * W), :], kernel, preferred_element_type=F32
    )
    for i, sum_row in enumerate(sum_rows):
        part = product[:, i * Z : i * Z + Z]
        if i and count == 1:
            break
        if i:
            part = jnp.where(first, part[W:], part[:-W])
        here = pl.ds(pl.multiple_of(sum_row * W, W), (count - i) * W)
        sum_ref[here, :] = sum_ref[here, :] + part


def inner_kernel(own_ref, psf_ref, sum_ref, meas_ref, rows_ref, taps_ref):
    core = lax.axis_index("core")
    blocks = turned_groups(own_ref, 4)
    fill_first_rows(blocks, rows_ref)
    rows_ref[264:344, :] = blocks[3][48:]
    for j in range(H + R):
        if j < 2 * R:
            spread_row(rows_ref, taps_ref, j * C, j + 3 * core)
        else:
            spread_row(rows_ref, taps_ref, 264 + (j - 2 * R) * C, j - 2 * R * core)
    for part, even_row, odd_row in ((blocks[2][:64], 0, 3), (blocks[0][4 * C : 4 * C + W], 4, 7), (blocks[3][:48], 5, 0)):
        row = even_row + (odd_row - even_row) * core
        meas_ref[pl.ds(pl.multiple_of(row * W, W), part.shape[0]), :] = decoded(part)
    sum_ref[...] = jnp.zeros(sum_ref.shape, F32)
    for k in range(R, -R - 1, -2):
        steps = range(k, max(k - 2, -R - 1), -1)
        add_products(
            taps_ref,
            psf_ref,
            sum_ref,
            [R + i * (1 - 2 * core) for i in steps],
            H + k,
            (R - k) * core,
            [(R - i) * (1 - core) for i in steps],
            core == 1,
        )


def ratio_kernel(inner_ref, meas_ref, next_ref, psf_ref, out_ref, rows_ref, taps_ref, sum_ref):
    core = lax.axis_index("core")
    even = core == 0
    blocks = turned_groups(next_ref, 3)
    fill_first_rows(blocks, rows_ref)
    for j in range(2 * R):
        spread_row(rows_ref, taps_ref, j * C, j)
    sum_ref[...] = inner_ref[...]
    for k in range(-R, R, 2):
        steps = (k, k + 1)
        add_products(
            taps_ref,
            psf_ref,
            sum_ref,
            [R + i * (1 - 2 * core) for i in steps],
            R - k,
            (R + k) * (1 - core),
            [(H + i) * core for i in steps],
            even,
        )
    here = pl.ds(pl.multiple_of(R * W * (1 - core), W), H * W)
    out_ref[here, :] = (meas_ref[...] / sum_ref[here, :]).astype(BF16)
    there = H * W * core
    for part, row in ((blocks[2][:64], 0), (blocks[0][4 * C : 4 * C + W], 4)):
        here = pl.ds(pl.multiple_of(there + row * W, W), part.shape[0])
        out_ref[here, :] = (decoded(part) / sum_ref[here, :]).astype(BF16)


def back_kernel(chip_ref, psf_ref, out_ref, rows_ref, sum_ref):
    first_row = lax.axis_index("core") * (H * W)
    for y in range(H + 2 * R):
        value = chip_ref[pl.ds(pl.multiple_of(first_row + y * W, W), W), :]
        for a in range(E):
            row = y + a - 2 * R
            if 0 <= row < H:
                rows_ref[row * W : row * W + W, a * 128 : a * 128 + 128] = value
    rows_ref[H * W : H * W + W, :] = jnp.ones((W, E * Z), BF16)
    weight = jnp.zeros((1, Z), F32)
    sums = [jnp.zeros((S, Z), F32) for _ in range(H)]
    gap = jnp.zeros((16, 2 * Z), F32)
    for y in range(H):
        sum_ref[y * 48 : y * 48 + 16, :] = gap
        sum_ref[y * 48 + 32 : y * 48 + 48, :] = gap
    for first in range(0, E, 2):
        pair = range(first, min(first + 2, E))
        kernel = jnp.concatenate(
            [psf_ref[a, first : first + len(pair)].reshape(len(pair) * Z, Z) for a in range(E)], axis=1
        )
        product = lax.dot_general(rows_ref[...], kernel, (((1,), (1,)), ((), ())), preferred_element_type=F32)
        for y in range(H):
            sum_ref[y * 48 + 16 : y * 48 + 32, : len(pair) * Z] = product[y * W : y * W + W]
        for i, b in enumerate(pair):
            weight = weight + product[H * W : H * W + 1, i * Z : i * Z + Z]
            for y in range(H):
                start = y * 48 + 16 - b
                sums[y] = sums[y] + sum_ref[start : start + S, i * Z : i * Z + Z]
    factor = SCALE / weight
    for g in range(2):
        share = (jnp.concatenate(sums[4 * g : 4 * g + 4], axis=0) * factor).T
        out_ref[:, :, g * 128 : g * 128 + 128] = share.reshape(TILES, 8, 128)


def final_kernel(parts_ref, vol_ref, mark_ref, out_ref):
    lane = lanes()
    for y in range(H):
        g, s = y // 4, y % 4
        turned = []
        for t in range(TILES):
            part = parts_ref[t, :, g * 128 : g * 128 + 128]
            shift = (W * t - R - S * s) % 128
            turned.append(pltpu.roll(part, shift, 1) if shift else part)
        for half in range(2):
            sums = [None, None]
            for t in range(TILES):
                start, stop = W * t - R - 128 * half, W * t + W + R - 128 * half
                start, stop = max(start, 0), min(stop, 128)
                if start >= stop:
                    continue
                before = sums[t % 2]
                sums[t % 2] = jnp.where(
                    (lane >= start) & (lane < stop), turned[t], 0.0 if before is None else before
                )
            here = slice(half * 128, half * 128 + 128)
            out_ref[:, y, here] = vol_ref[:, y, here] * ((sums[0] + sums[1]) * (1 / SCALE))


def body(volume, measured, point_spread):
    mark = pl.pallas_call(
        mark_kernel,
        out_shape=jax.ShapeDtypeStruct((8, 128), F32),
        out_specs=VM,
        cost_estimate=pl.CostEstimate(flops=20_000_000_000, bytes_accessed=2**20, transcendentals=0),
        name="mark",
    )()
    volume_first, mark = lax.optimization_barrier((volume, mark))
    packed = pl.pallas_call(
        pack_kernel,
        out_shape=jax.ShapeDtypeStruct((TILES, 8, 512), F32),
        in_specs=[VM] * 2,
        out_specs=VM,
        compiler_params=PARAMS,
        cost_estimate=pl.CostEstimate(flops=20_000_000_000, bytes_accessed=2**20, transcendentals=0),
        name="pack",
    )(lax.all_gather(volume_first, "core"), measured)
    own = lax.all_to_all(packed.astype(F16), "depth", 0, 0, tiled=True)
    tile = ("pair", "core")
    count = lax.axis_size(tile)
    pairs = [(i, i + 1) for i in range(1, count - 1, 2)] + [(i, i - 1) for i in range(2, count, 2)]
    beyond = lax.ppermute(own[:, :, :384], tile, pairs)
    rows = H + R
    scratch = [pltpu.VMEM((rows * C + 14, Z), F32), pltpu.VMEM((rows * W, E * Z), BF16)]
    inner, near = pl.pallas_call(
        inner_kernel,
        out_shape=[jax.ShapeDtypeStruct((rows * W, Z), F32), jax.ShapeDtypeStruct((H * W, Z), F32)],
        in_specs=[VM] * 2,
        out_specs=[VM] * 2,
        scratch_shapes=scratch,
        compiler_params=PARAMS,
        cost_estimate=pl.CostEstimate(flops=2 * 88 * W * E * Z * Z, bytes_accessed=2**22, transcendentals=0),
        name="inner",
    )(own.astype(F32), point_spread)
    ratio = pl.pallas_call(
        ratio_kernel,
        out_shape=jax.ShapeDtypeStruct((rows * W, Z), BF16),
        in_specs=[VM] * 4,
        out_specs=VM,
        scratch_shapes=[*scratch, pltpu.VMEM((rows * W, Z), F32)],
        compiler_params=PARAMS,
        name="ratio",
    )(inner, near, beyond.astype(F32), point_spread)
    chip_ratio = lax.all_gather(ratio, "core", tiled=True)
    shares = pl.pallas_call(
        back_kernel,
        out_shape=jax.ShapeDtypeStruct((TILES, 8, H * S), F32),
        in_specs=[VM] * 2,
        out_specs=VM,
        scratch_shapes=[
            pltpu.VMEM((H * W + W, E * Z), BF16),
            pltpu.VMEM((H * 48, 2 * Z), F32),
        ],
        compiler_params=PARAMS,
        name="back",
    )(chip_ratio, point_spread)
    parts = lax.all_to_all(shares.astype(F16), "depth", 0, 0, tiled=True).astype(F32)
    return pl.pallas_call(
        final_kernel,
        out_shape=jax.ShapeDtypeStruct(volume.shape, F32),
        in_specs=[VM, VM, pl.BlockSpec(memory_space=pl.ANY)],
        out_specs=VM,
        compiler_params=PARAMS,
        name="final",
    )(parts, volume, mark)


def solution(mesh):
    depth, tile = mesh.devices.shape
    split = Mesh(mesh.devices.reshape(depth, tile // 2, 2), ("depth", "pair", "core"))
    spec = P("depth", ("pair", "core"), None)
    return jax.shard_map(body, mesh=split, in_specs=(spec, spec, P()), out_specs=spec, check_vma=False)
```

```python
import jax
import jax.numpy as jnp
from jax import lax
from jax.experimental import pallas as pl
from jax.experimental.pallas import tpu as pltpu
from jax.sharding import Mesh
from jax.sharding import PartitionSpec as P

R = 5
E = 11
Z = 128
TILES = 16
W = 16
H = 8
C = 26
S = 32
SCALE = 8.0
F32 = jnp.float32
BF16 = jnp.bfloat16
F16 = jnp.float16
VM = pl.BlockSpec(memory_space=pltpu.VMEM)
PARAMS = pltpu.CompilerParams(vmem_limit_bytes=40 * 1024 * 1024)


def lanes(shape=(8, 128)):
    return lax.broadcasted_iota(jnp.int32, shape, 1)


VOLUME_AT = [(0, C * i) for i in range(4)] + [(1, C * i) for i in range(4)]
VOLUME_AT += [(2, 64 + C * i) for i in range(2)] + [(3, 48 + C * i) for i in range(3)]
MEASURED_AT = [(2, W * i) for i in range(4)] + [(0, 4 * C)] + [(3, W * i) for i in range(3)]


def mark_kernel(out_ref):
    out_ref[0] = 0


def pack_kernel(vol_ref, meas_ref, out_ref):
    even = lax.axis_index("core") == 0
    lane = lanes()
    rows = {}
    rolled = {}

    def volume_row(j, half):
        here = slice(half * 128, half * 128 + 128)
        odd = j + 6 if j < 2 * R else j - 7
        a, b = [vol_ref[r // H, :, r % H, here] for r in (j, odd)]
        return jnp.where(even, a, b).astype(BF16).astype(F32)

    def measured_row(j, half):
        here = slice(half * 128, half * 128 + 128)
        odd = j + 3 if j < R else j - R
        part = jnp.where(even, meas_ref[:, j, here], meas_ref[:, odd, here])
        part = part * part
        return part * part

    def turned(make, j, half, shift):
        name = (make, j, half)
        if name not in rows:
            rows[name] = make(j, half)
        shift = shift % 128
        if (name, shift) not in rolled:
            rolled[name, shift] = pltpu.roll(rows[name], shift, 1) if shift else rows[name]
        return rolled[name, shift]

    def window(t, j, at):
        start = W * t - R
        low, high = max(start, 0) // 128, min(start + C - 1, 255) // 128
        value = turned(volume_row, j, low, at - start)
        if high != low:
            value = jnp.where(lane - at < 128 - start, value, turned(volume_row, j, high, at - start))
        if start < 0:
            value = jnp.where(lane - at < -start, 0.0, value)
        if start + C > 256:
            value = jnp.where(lane - at < 256 - start, value, 0.0)
        return value

    for t in range(TILES):
        for g in range(4):
            parts = [(at, window(t, j, at)) for j, (where, at) in enumerate(VOLUME_AT) if where == g]
            parts += [
                (at, turned(measured_row, j, t // 8, at - W * t)) for j, (where, at) in enumerate(MEASURED_AT) if where == g
            ]
            parts.sort(key=lambda part: part[0])
            value = parts[0][1]
            for at, part in parts[1:]:
                value = jnp.where(lane < at, value, part)
            out_ref[t, :, g * 128 : g * 128 + 128] = value


def turned_groups(packed_ref, count):
    return [packed_ref[:, :, g * 128 : g * 128 + 128].reshape(Z, 128).T for g in range(count)]


def decoded(value):
    return jnp.where(value > 0.0, jnp.sqrt(jnp.sqrt(value)), 0.0)


def fill_first_rows(blocks, rows_ref):
    rows_ref[: 4 * C, :] = blocks[0][: 4 * C]
    rows_ref[4 * C : 8 * C, :] = blocks[1][: 4 * C]
    rows_ref[8 * C : 8 * C + 56, :] = blocks[2][64:120]


def spread_row(rows_ref, taps_ref, start, row):
    here = pl.ds(pl.multiple_of(row * W, W), W)
    for b in range(E):
        taps_ref[here, b * 128 : b * 128 + 128] = rows_ref[start + b : start + b + W, :].astype(BF16)


def add_products(taps_ref, psf_ref, sum_ref, offsets, count, taps_row, sum_rows, first):
    kernel = jnp.concatenate([psf_ref[offset].reshape(E * Z, Z) for offset in offsets], axis=1)
    product = jnp.dot(
        taps_ref[pl.ds(pl.multiple_of(taps_row * W, W), count * W), :], kernel, preferred_element_type=F32
    )
    for i, sum_row in enumerate(sum_rows):
        part = product[:, i * Z : i * Z + Z]
        if i and count == 1:
            break
        if i:
            part = jnp.where(first, part[W:], part[:-W])
        here = pl.ds(pl.multiple_of(sum_row * W, W), (count - i) * W)
        sum_ref[here, :] = sum_ref[here, :] + part


def inner_kernel(own_ref, psf_ref, sum_ref, meas_ref, rows_ref, taps_ref):
    core = lax.axis_index("core")
    blocks = turned_groups(own_ref, 4)
    fill_first_rows(blocks, rows_ref)
    rows_ref[264:344, :] = blocks[3][48:]
    for j in range(H + R):
        if j < 2 * R:
            spread_row(rows_ref, taps_ref, j * C, j + 3 * core)
        else:
            spread_row(rows_ref, taps_ref, 264 + (j - 2 * R) * C, j - 2 * R * core)
    for part, even_row, odd_row in ((blocks[2][:64], 0, 3), (blocks[0][4 * C : 4 * C + W], 4, 7), (blocks[3][:48], 5, 0)):
        row = even_row + (odd_row - even_row) * core
        meas_ref[pl.ds(pl.multiple_of(row * W, W), part.shape[0]), :] = decoded(part)
    sum_ref[...] = jnp.zeros(sum_ref.shape, F32)
    for k in range(R, -R - 1, -2):
        steps = range(k, max(k - 2, -R - 1), -1)
        add_products(
            taps_ref,
            psf_ref,
            sum_ref,
            [R + i * (1 - 2 * core) for i in steps],
            H + k,
            (R - k) * core,
            [(R - i) * (1 - core) for i in steps],
            core == 1,
        )


def ratio_kernel(inner_ref, meas_ref, next_ref, psf_ref, out_ref, rows_ref, taps_ref, sum_ref):
    core = lax.axis_index("core")
    even = core == 0
    blocks = turned_groups(next_ref, 3)
    fill_first_rows(blocks, rows_ref)
    for j in range(2 * R):
        spread_row(rows_ref, taps_ref, j * C, j)
    sum_ref[...] = inner_ref[...]
    for k in range(-R, R, 2):
        steps = (k, k + 1)
        add_products(
            taps_ref,
            psf_ref,
            sum_ref,
            [R + i * (1 - 2 * core) for i in steps],
            R - k,
            (R + k) * (1 - core),
            [(H + i) * core for i in steps],
            even,
        )
    here = pl.ds(pl.multiple_of(R * W * (1 - core), W), H * W)
    out_ref[here, :] = (meas_ref[...] / sum_ref[here, :]).astype(BF16)
    there = H * W * core
    for part, row in ((blocks[2][:64], 0), (blocks[0][4 * C : 4 * C + W], 4)):
        here = pl.ds(pl.multiple_of(there + row * W, W), part.shape[0])
        out_ref[here, :] = (decoded(part) / sum_ref[here, :]).astype(BF16)


def back_kernel(chip_ref, psf_ref, out_ref, rows_ref, sum_ref):
    first_row = lax.axis_index("core") * (H * W)
    for y in range(H + 2 * R):
        value = chip_ref[pl.ds(pl.multiple_of(first_row + y * W, W), W), :]
        for a in range(E):
            row = y + a - 2 * R
            if 0 <= row < H:
                rows_ref[row * W : row * W + W, a * 128 : a * 128 + 128] = value
    rows_ref[H * W : H * W + W, :] = jnp.ones((W, E * Z), BF16)
    sum_ref[...] = jnp.zeros((H * S, Z), F32)
    weight = jnp.zeros((1, Z), F32)
    for first in range(0, E, 2):
        pair = range(first, min(first + 2, E))
        kernel = jnp.concatenate(
            [psf_ref[a, first : first + len(pair)].reshape(len(pair) * Z, Z) for a in range(E)], axis=1
        )
        product = lax.dot_general(rows_ref[...], kernel, (((1,), (1,)), ((), ())), preferred_element_type=F32)
        for i, b in enumerate(pair):
            part = product[:, i * Z : i * Z + Z]
            for y in range(H):
                here = slice(y * S + b, y * S + b + W)
                sum_ref[here, :] = sum_ref[here, :] + part[y * W : y * W + W]
            weight = weight + part[H * W : H * W + 1]
    factor = SCALE / weight
    for g in range(2):
        share = (sum_ref[g * 128 : g * 128 + 128, :] * factor).T
        out_ref[:, :, g * 128 : g * 128 + 128] = share.reshape(TILES, 8, 128)


def final_kernel(parts_ref, vol_ref, mark_ref, out_ref):
    lane = lanes()
    for y in range(H):
        g, s = y // 4, y % 4
        turned = []
        for t in range(TILES):
            part = parts_ref[t, :, g * 128 : g * 128 + 128]
            shift = (W * t - R - S * s) % 128
            turned.append(pltpu.roll(part, shift, 1) if shift else part)
        for half in range(2):
            sums = [None, None]
            for t in range(TILES):
                start, stop = W * t - R - 128 * half, W * t + W + R - 128 * half
                start, stop = max(start, 0), min(stop, 128)
                if start >= stop:
                    continue
                before = sums[t % 2]
                sums[t % 2] = jnp.where(
                    (lane >= start) & (lane < stop), turned[t], 0.0 if before is None else before
                )
            here = slice(half * 128, half * 128 + 128)
            out_ref[:, y, here] = vol_ref[:, y, here] * ((sums[0] + sums[1]) * (1 / SCALE))


def body(volume, measured, point_spread):
    mark = pl.pallas_call(
        mark_kernel,
        out_shape=jax.ShapeDtypeStruct((1,), jnp.int32),
        out_specs=pl.BlockSpec(memory_space=pltpu.SMEM),
        cost_estimate=pl.CostEstimate(flops=20_000_000_000, bytes_accessed=2**20, transcendentals=0),
        name="mark",
    )()
    volume_first, mark = lax.optimization_barrier((volume, mark))
    packed = pl.pallas_call(
        pack_kernel,
        out_shape=jax.ShapeDtypeStruct((TILES, 8, 512), F32),
        in_specs=[VM] * 2,
        out_specs=VM,
        compiler_params=PARAMS,
        cost_estimate=pl.CostEstimate(flops=20_000_000_000, bytes_accessed=2**20, transcendentals=0),
        name="pack",
    )(lax.all_gather(volume_first, "core"), measured)
    own = lax.all_to_all(packed.astype(F16), "depth", 0, 0, tiled=True)
    tile = ("pair", "core")
    count = lax.axis_size(tile)
    pairs = [(i, i + 1) for i in range(1, count - 1, 2)] + [(i, i - 1) for i in range(2, count, 2)]
    beyond = lax.ppermute(own[:, :, :384], tile, pairs)
    rows = H + R
    scratch = [pltpu.VMEM((rows * C + 14, Z), F32), pltpu.VMEM((rows * W, E * Z), BF16)]
    inner, near = pl.pallas_call(
        inner_kernel,
        out_shape=[jax.ShapeDtypeStruct((rows * W, Z), F32), jax.ShapeDtypeStruct((H * W, Z), F32)],
        in_specs=[VM] * 2,
        out_specs=[VM] * 2,
        scratch_shapes=scratch,
        compiler_params=PARAMS,
        cost_estimate=pl.CostEstimate(flops=2 * 88 * W * E * Z * Z, bytes_accessed=2**22, transcendentals=0),
        name="inner",
    )(own.astype(F32), point_spread)
    ratio = pl.pallas_call(
        ratio_kernel,
        out_shape=jax.ShapeDtypeStruct((rows * W, Z), BF16),
        in_specs=[VM] * 4,
        out_specs=VM,
        scratch_shapes=[*scratch, pltpu.VMEM((rows * W, Z), F32)],
        compiler_params=PARAMS,
        name="ratio",
    )(inner, near, beyond.astype(F32), point_spread)
    chip_ratio = lax.all_gather(ratio, "core", tiled=True)
    shares = pl.pallas_call(
        back_kernel,
        out_shape=jax.ShapeDtypeStruct((TILES, 8, H * S), F32),
        in_specs=[VM] * 2,
        out_specs=VM,
        scratch_shapes=[
            pltpu.VMEM((H * W + W, E * Z), BF16),
            pltpu.VMEM((H * S, Z), F32),
        ],
        compiler_params=PARAMS,
        name="back",
    )(chip_ratio, point_spread)
    parts = lax.all_to_all(shares.astype(F16), "depth", 0, 0, tiled=True).astype(F32)
    return pl.pallas_call(
        final_kernel,
        out_shape=jax.ShapeDtypeStruct(volume.shape, F32),
        in_specs=[VM, VM, pl.BlockSpec(memory_space=pltpu.SMEM)],
        out_specs=VM,
        compiler_params=PARAMS,
        name="final",
    )(parts, volume, mark)


def solution(mesh):
    depth, tile = mesh.devices.shape
    split = Mesh(mesh.devices.reshape(depth, tile // 2, 2), ("depth", "pair", "core"))
    spec = P("depth", ("pair", "core"), None)
    return jax.shard_map(body, mesh=split, in_specs=(spec, spec, P()), out_specs=spec, check_vma=False)
```
